128 devices in a mesh: wide: 16 (over x_lo, y, core), narrow: 8 (over x_hi, z).
Axes of the slice: x: 4 (x_hi: 2, x_lo: 2; x = x_hi * 2 + x_lo), y: 4, z: 4, core: 2. Of those that a mesh axis runs over, the one named last changes fastest.
Arguments:
- base: float32 [1, 16, 2, 8, 512, 512], P(None, 'wide', None, 'narrow'), may hold values from -3.7 to 8
- block_mask: int32 [16, 16], replicated, may hold values 0 or 1
- heads: float32 [8192], P('narrow'), may hold values from -6 to 6
- coef: float32 [9000], replicated, may hold values from 0.3 to 1.2
- weir_node: int32 [9000], replicated, may hold values from 0 to 4095
- weir_cell: int32 [9000], replicated, may hold values from 4096 to 8191
Outputs:
- factored: float32 [1, 16, 2, 8, 512, 512], P(None, 'wide', None, 'narrow')
The draws below stay inside these ranges and needn't reach their ends.
All inputs are finite; a program needn't handle non-finite values.
Results may differ from the reference program's by a relative error of at most 0.0001.
Values sent between devices are 32-bit elements; how exact they have to be, the bound alone decides.
A program may use at most 64 MiB of HBM per device.

```python
import math
import jax
import jax.numpy as jnp
from jax import lax

B = 512
BLK = 1
PANELS = 2
NS_STEPS = 6
WEIRS = 9000
GRID_ROWS = 16
GRID_COLS = 8
NB = 16
BLKC = 2
N = 8192


def draw_base(key, part):
    key = jax.random.fold_in(key, 11)
    first, second = jax.random.split(key)
    shape = (BLK, GRID_ROWS, BLKC, GRID_COLS, B, B)
    rowa = lax.broadcasted_iota(jnp.int32, (BLK, 1, 1, 1, 1, 1), 0)
    rowr = lax.broadcasted_iota(jnp.int32, (1, GRID_ROWS, 1, 1, 1, 1), 1)
    colb = lax.broadcasted_iota(jnp.int32, (1, 1, BLKC, 1, 1, 1), 2)
    colc = lax.broadcasted_iota(jnp.int32, (1, 1, 1, GRID_COLS, 1, 1), 3)
    inner_p = lax.broadcasted_iota(jnp.int32, (1, 1, 1, 1, B, 1), 4)
    inner_q = lax.broadcasted_iota(jnp.int32, (1, 1, 1, 1, 1, B), 5)
    same = rowa * GRID_ROWS + rowr == colb * GRID_COLS + colc
    lead_shape = (BLK, GRID_ROWS, 1, 1, B, 1)
    noise = jnp.clip(jax.random.normal(first, shape, jnp.float32), -4.0, 4.0)
    lead = 4.0 * jnp.exp(jax.random.uniform(second, lead_shape, jnp.float32) * math.log(2.0))
    couple = -0.45 * jnp.sqrt(lead * jnp.swapaxes(lead, 4, 5))
    distance = jnp.abs(inner_p - inner_q)
    spread = jnp.where(same, 0.06, 0.08) / math.sqrt(B)
    chain = jnp.where(distance == 1, couple, 0.0)
    inside = jnp.where(distance == 0, lead, chain + noise * spread)
    return jnp.where(same, inside, noise * spread).astype(jnp.float32)


def touch_ends(entries, own_key, least, high):
    longest = entries.shape.index(max(entries.shape))
    spots = []
    for shift in (0, 1):
        where = [jax.random.randint(jax.random.fold_in(own_key, axis), (), 0, length) for axis, length in enumerate(entries.shape)]
        where[longest] = (where[longest] + shift) % entries.shape[longest]
        spots.append(tuple(where))
    return entries.at[spots[0]].set(least).at[spots[1]].set(high)


def block_levels(stream_key, extent, cuts, least, largest):
    gain = 1.0
    for position, blocks in cuts:
        heights = jax.random.uniform(jax.random.fold_in(jax.random.fold_in(stream_key, 6), position), (blocks,), jnp.float32, least / len(cuts), largest / len(cuts))
        gain = gain * jnp.repeat(jnp.exp(heights), extent[position] // blocks).reshape((-1,) + (1,) * (len(extent) - 1 - position))
    return gain


def bell_draw(own_key, extent, scale, reach, pieces=(), kind=jnp.bfloat16):
    gain = block_levels(own_key, extent, pieces, -0.22, 0.18) if pieces else 1.0
    array = jax.random.normal(own_key, extent, jnp.float32) * scale * gain
    return jnp.minimum(jnp.maximum(array, -reach), reach).astype(kind)


def setup_inputs(seed: int = 0) -> dict:
    streams_of = jax.random.split(jax.random.key(seed), 7)
    base = draw_base(jax.random.fold_in(streams_of[6], 71), 0)
    block_mask = touch_ends((jax.random.randint(streams_of[1], (NB, NB), 0, 2) < 1).astype(jnp.int32), jax.random.fold_in(streams_of[1], 1), 0, 1)
    heads = bell_draw(streams_of[2], (N,), 1.0, 6.0, ((0, 8),), jnp.float32)
    coef = jnp.clip(jnp.exp(jax.random.uniform(streams_of[3], (WEIRS,), jnp.float32, math.log(0.3), math.log(1.2))), 0.3, 1.2)
    weir_node = touch_ends(jax.random.randint(streams_of[4], (WEIRS,), 0, N // 2), jax.random.fold_in(streams_of[4], 1), 0, (N // 2) - 1).astype(jnp.int32)
    weir_cell = touch_ends(jax.random.randint(streams_of[5], (WEIRS,), N // 2, N), jax.random.fold_in(streams_of[5], 1), N // 2, N - 1).astype(jnp.int32)
    return dict(base=base, block_mask=block_mask, heads=heads, coef=coef, weir_node=weir_node, weir_cell=weir_cell)


def newton_schulz(block):
    approx = jnp.diag(1.0 / jnp.diagonal(block))
    for step in range(NS_STEPS):
        inner = jnp.dot(block, approx, precision=lax.Precision.HIGHEST)
        approx = 2.0 * approx - jnp.dot(approx, inner, precision=lax.Precision.HIGHEST)
    return approx

def reference(base, block_mask, heads, coef, weir_node, weir_cell):
    matrix = base.reshape(NB, NB, B, B)
    blockid = jnp.arange(NB, dtype=jnp.int32)
    keep = (block_mask != 0) | (blockid[:, None] == blockid[None, :])
    matrix = matrix * keep.astype(matrix.dtype)[:, :, None, None]
    drop = heads[weir_node] - heads[weir_cell]
    flux = 1.5 * coef * jnp.sqrt(drop * drop + 0.01)
    rows = jnp.concatenate([weir_node, weir_cell, weir_node, weir_cell]).astype(jnp.int32)
    cols = jnp.concatenate([weir_node, weir_cell, weir_cell, weir_node]).astype(jnp.int32)
    vals = jnp.concatenate([flux, flux, -flux, -flux])
    matrix = matrix.at[rows // B, cols // B, rows % B, cols % B].add(vals)
    for k in range(PANELS):
        inverse = newton_schulz(matrix[k, k])
        later = (blockid > k)[:, None, None]
        product = jnp.einsum('pq,jqs->jps', inverse, matrix[k], precision=lax.Precision.HIGHEST)
        scaled = jnp.where(later, product, jnp.zeros_like(product))
        matrix = matrix.at[k].set(jnp.where(later, scaled, matrix[k]))

        def update_row(index, current):
            row = lax.dynamic_index_in_dim(current, index, 0, keepdims=False)
            term = jnp.einsum('ps,jsq->jpq', row[k], scaled, precision=lax.Precision.HIGHEST)
            return lax.dynamic_update_index_in_dim(current, row - term, index, 0)
        matrix = lax.fori_loop(k + 1, NB, update_row, matrix)
    return matrix.reshape(base.shape)
```

```python
import functools

import jax
import jax.numpy as jnp
from jax import lax
from jax.experimental import pallas as pl
from jax.experimental.pallas import tpu as pltpu
from jax.sharding import PartitionSpec as P

NS_STEPS = 6
B = 512
ROWS = 72
LANES = 128
MESH = pl.DeviceIdType.MESH
F32 = jnp.float32
BF16 = jnp.bfloat16
VMEM_LIMIT = 56 * 2**20
TREE_ROWS = ((0, 88), (88, 88), (176, 80))


def split(x):
    high = x.astype(BF16)
    return high, (x - high.astype(F32)).astype(BF16)


def dot(a, b):
    return jnp.dot(a, b, preferred_element_type=F32)


def dot_nt(a, b):
    return lax.dot_general(a, b, (((1,), (1,)), ((), ())), preferred_element_type=F32)


def product(ah, al, bh, bl):
    return dot(ah, bh) + dot(ah, bl) + dot(al, bh)


def gather_heads_kernel(mine_ref, every_ref, send_sem, recv_sem):
    r = lax.axis_index("wide")
    c = lax.axis_index("narrow")
    count = 8
    barrier = pltpu.get_barrier_semaphore()
    for hop in range(1, count):
        pl.semaphore_signal(barrier, inc=1, device_id=(r, lax.rem(c + hop, count)), device_id_type=MESH)
    pl.semaphore_wait(barrier, count - 1)
    place = pl.ds(pl.multiple_of(c * 8, 8), 8)
    copies = []
    for hop in range(1, count):
        copy = pltpu.make_async_remote_copy(
            src_ref=mine_ref,
            dst_ref=every_ref.at[place],
            send_sem=send_sem.at[hop],
            recv_sem=recv_sem.at[hop],
            device_id=(r, lax.rem(c + hop, count)),
            device_id_type=MESH,
        )
        copy.start()
        copies.append(copy)
    every_ref[place] = mine_ref[...]
    for copy in copies:
        copy.wait()


def gather_heads(heads):
    return pl.pallas_call(
        gather_heads_kernel,
        out_shape=jax.ShapeDtypeStruct((64, LANES), F32),
        in_specs=[pl.BlockSpec(memory_space=pltpu.VMEM)],
        out_specs=pl.BlockSpec(memory_space=pltpu.VMEM),
        scratch_shapes=[pltpu.SemaphoreType.DMA((8,)), pltpu.SemaphoreType.DMA((8,))],
        compiler_params=pltpu.CompilerParams(collective_id=0, has_side_effects=True),
        name="gather_heads",
    )(heads.reshape(8, LANES))


def lookup(table_ref, first, index):
    high = lax.shift_right_logical(index, 7) - first
    low = jnp.bitwise_and(index, 127)
    found = jnp.zeros(index.shape, F32)
    for t in range(32):
        row = jnp.broadcast_to(table_ref[pl.ds(first + t, 1), :], index.shape)
        picked = jnp.take_along_axis(row, low, axis=1, mode="promise_in_bounds")
        found = jnp.where(high == t, picked, found)
    return found


def pieces(x):
    high = x.astype(BF16).astype(F32)
    rest = x - high
    middle = rest.astype(BF16).astype(F32)
    return high, middle, rest - middle


def weirs_kernel(mask_ref, base_ref, heads_ref, coef_ref, node_ref, cell_ref, out_ref, code_ref, flux_ref):
    r = lax.axis_index("wide")
    c = lax.axis_index("narrow")
    upper = r < 8
    for j in range(2):
        col = c + 8 * j
        keep = jnp.where((mask_ref[r, col] != 0) | (r == col), 1.0, 0.0).astype(F32)
        out_ref[j] = base_ref[j] * keep
    node = node_ref[...]
    cell = cell_ref[...]
    drop = lookup(heads_ref, 0, node) - lookup(heads_ref, 32, cell)
    flux = 1.5 * coef_ref[...] * jnp.sqrt(drop * drop + 0.01)
    row = jnp.where(upper, node, cell)
    col = jnp.where(upper, cell, node)
    mine = lax.shift_right_logical(row, 9) == r
    low_row = jnp.bitwise_and(row, 511)

    target = jnp.where(upper, c + 8, c)
    slot = jnp.where(upper, 1, 0)
    hit = jnp.where(mine & (lax.shift_right_logical(col, 9) == target), 1, 0)
    code = low_row * 512 + jnp.bitwise_and(col, 511)
    steps = jnp.max(jnp.sum(hit.astype(F32), axis=0, keepdims=True)).astype(jnp.int32)
    code_ref[...] = jnp.zeros(code_ref.shape, jnp.int32)
    flux_ref[...] = jnp.zeros(flux_ref.shape, F32)
    place = lax.broadcasted_iota(jnp.int32, (ROWS, LANES), 0)

    def extract(s, left):
        first = jnp.min(jnp.where(left != 0, place, ROWS), axis=0, keepdims=True)
        now = place == first
        code_ref[pl.ds(s, 1), :] = jnp.sum(jnp.where(now, code, 0), axis=0, keepdims=True)
        flux_ref[pl.ds(s, 1), :] = jnp.sum(jnp.where(now, flux, 0.0), axis=0, keepdims=True)
        return jnp.where(now, 0, left)

    lax.fori_loop(0, steps, extract, hit)

    def scatter(b, carry):
        rows = pl.ds(pl.multiple_of(b * 8, 8), 8)
        codes = code_ref[rows]
        parts = pieces(flux_ref[rows])
        here = lax.broadcasted_iota(jnp.int32, (B, LANES), 0)
        row_of = lax.shift_right_logical(codes, 9)
        col_of = jnp.bitwise_and(codes, 511)
        right = jnp.concatenate(
            [jnp.where(here == col_of[s : s + 1], 1.0, 0.0).astype(BF16) for s in range(8)], axis=1
        )
        total = jnp.zeros((B, B), F32)
        for part in parts:
            left = jnp.concatenate(
                [jnp.where(here == row_of[s : s + 1], part[s : s + 1], 0.0).astype(BF16) for s in range(8)],
                axis=1,
            )
            total = total + dot_nt(left, right)
        out_ref[slot] = out_ref[slot] - total
        return carry

    lax.fori_loop(0, lax.div(steps + 7, 8), scatter, 0)

    @pl.when(c == lax.rem(r, 8))
    def _():
        own = jnp.where(mine, flux, 0.0)
        parts = pieces(own)
        high = lax.shift_right_logical(low_row, 7)
        low = jnp.bitwise_and(low_row, 127)
        here8 = lax.broadcasted_iota(jnp.int32, (8, LANES), 0)
        here128 = lax.broadcasted_iota(jnp.int32, (LANES, LANES), 0)
        total = jnp.zeros((24, LANES), F32)
        for g in range(ROWS // 8):
            ones = []
            lefts = []
            for s in range(8 * g, 8 * g + 8):
                ones.append(jnp.where(here128 == low[s : s + 1], 1.0, 0.0).astype(BF16))
                at = here8 == high[s : s + 1]
                lefts.append(
                    jnp.concatenate([jnp.where(at, part[s : s + 1], 0.0) for part in parts], axis=0).astype(BF16)
                )
            total = total + dot_nt(jnp.concatenate(lefts, axis=1), jnp.concatenate(ones, axis=1))
        diagonal = total[0:8] + total[8:16] + total[16:24]
        eye = here128 == lax.broadcasted_iota(jnp.int32, (LANES, LANES), 1)
        which = jnp.where(upper, 0, 1)
        for t in range(4):
            part = pl.ds(t * LANES, LANES)
            out_ref[which, part, part] = out_ref[which, part, part] + jnp.where(eye, diagonal[t : t + 1], 0.0)


def add_weirs(base, block_mask, every_head, coef, weir_node, weir_cell):
    pad = ROWS * LANES - coef.shape[0]
    coef = jnp.pad(coef, (0, pad)).reshape(ROWS, LANES)
    node = jnp.pad(weir_node, (0, pad)).reshape(ROWS, LANES)
    cell = jnp.pad(weir_cell, (0, pad), constant_values=4096).reshape(ROWS, LANES)
    vmem = pl.BlockSpec(memory_space=pltpu.VMEM)
    return pl.pallas_call(
        weirs_kernel,
        out_shape=jax.ShapeDtypeStruct((2, B, B), F32),
        in_specs=[pl.BlockSpec(memory_space=pltpu.SMEM)] + [vmem] * 5,
        out_specs=vmem,
        scratch_shapes=[pltpu.VMEM((ROWS, LANES), jnp.int32), pltpu.VMEM((ROWS, LANES), F32)],
        compiler_params=pltpu.CompilerParams(vmem_limit_bytes=VMEM_LIMIT),
        name="add_weirs",
    )(block_mask, base, every_head, coef, node, cell)


def eliminate_kernel(
    a_ref, out_ref, side, panel, pivot, ph, pl_, sh, sl, xf, wide_send, wide_recv, pair_recv, side_send, side_recv
):
    r = lax.axis_index("wide")
    c = lax.axis_index("narrow")
    core = lax.rem(r, 2)
    y = lax.rem(lax.div(r, 2), 4)
    x = lax.div(r, 8)
    z = lax.rem(c, 4)
    far = lax.div(c, 4)
    up = (x * 8 + lax.rem(y + 1, 4) * 2 + core, c)
    down = (x * 8 + lax.rem(y + 3, 4) * 2 + core, c)
    across = ((1 - x) * 8 + y * 2 + core, c)
    pair = (x * 8 + y * 2 + 1 - core, c)
    ahead = (r, far * 4 + lax.rem(z + 1, 4))
    behind = (r, far * 4 + lax.rem(z + 3, 4))
    over = (r, (1 - far) * 4 + z)
    near_x = x == 0

    barrier = pltpu.get_barrier_semaphore()
    for peer in (up, down, across, pair, ahead, behind, over):
        pl.semaphore_signal(barrier, inc=1, device_id=peer, device_id_type=MESH)
    pl.semaphore_wait(barrier, 7)

    def either(*terms):
        out = terms[0]
        for term in terms[1:]:
            out = out | term
        return out

    far_x = x == 1
    tree_up = (either(near_x & (y < 3), far_x & (y == 2)), far_x & (y == 3), far_x & (y < 2))
    tree_down = (far_x & (y == 1), either(near_x & (y != 1), far_x & (y >= 2)), far_x & (y == 0))
    tree_across = (
        near_x & ((y == 1) | (y == 2)),
        near_x & (y == 3),
        either(near_x & (y == 0), far_x & (y > 0)),
    )

    def wide_chunk(half, tree):
        start, size = TREE_ROWS[tree]
        return panel.at[core, lax.div(half, 2), pl.ds(pl.multiple_of(lax.rem(half, 2) * 256 + start, 8), size)]

    def wide_copy(half, tree, way, target):
        chunk = wide_chunk(half, tree)
        at = half * 3 + tree
        return pltpu.make_async_remote_copy(
            src_ref=chunk,
            dst_ref=chunk,
            send_sem=wide_send.at[at, way],
            recv_sem=(pair_recv if way == 3 else wide_recv).at[at],
            device_id=target,
            device_id_type=MESH,
        )

    def each_way(half, tree, act):
        for way, (target, when) in enumerate(
            ((up, tree_up[tree]), (down, tree_down[tree]), (across, tree_across[tree]))
        ):

            @pl.when(when)
            def _():
                act(wide_copy(half, tree, way, target))

        act(wide_copy(half, tree, 3, pair))

    def wide_start(half):
        for tree in range(3):
            each_way(half, tree, lambda copy: copy.start())

    def wide_relay(half):
        for tree in range(3):
            wide_copy(half, tree, 0, up).wait_recv()
            each_way(half, tree, lambda copy: copy.start())

    def pair_wait(first, last):
        def one(half, carry):
            for tree in range(3):
                start, size = TREE_ROWS[tree]
                rows = pl.ds(pl.multiple_of(lax.rem(half, 2) * 256 + start, 8), size)
                chunk = panel.at[1 - core, lax.div(half, 2), rows]
                pltpu.make_async_remote_copy(
                    src_ref=chunk,
                    dst_ref=chunk,
                    send_sem=wide_send.at[half * 3 + tree, 3],
                    recv_sem=pair_recv.at[half * 3 + tree],
                    device_id=pair,
                    device_id_type=MESH,
                ).wait_recv()
            return carry

        lax.fori_loop(first, last, one, 0)

    def side_copy(s, q, way, target):
        chunk = side.at[s, pl.ds(q * 128, 128)]
        return pltpu.make_async_remote_copy(
            src_ref=chunk,
            dst_ref=chunk,
            send_sem=side_send.at[s, q, way],
            recv_sem=side_recv.at[s, q],
            device_id=target,
            device_id_type=MESH,
        )

    near = far == 0
    away = far == 1

    def side_ways(s, q):
        rel = lax.rem(z + 4 - s, 4)
        if q < 2:
            ahead_near, behind_near = rel < 3, None
        else:
            ahead_near, behind_near = None, rel != 1
        if q % 2 == 0:
            ahead_far, behind_far = (rel == q) | (rel == (q + 1) % 4), rel == q
        else:
            ahead_far, behind_far = rel == q, (rel == q) | (rel == (q + 3) % 4)
        go_ahead = away & ahead_far if ahead_near is None else (near & ahead_near) | (away & ahead_far)
        go_behind = away & behind_far if behind_near is None else (near & behind_near) | (away & behind_far)
        return ((ahead, go_ahead), (behind, go_behind), (over, near & (rel == q)))

    def side_each(s, q, act):
        for way, (target, when) in enumerate(side_ways(s, q)):

            @pl.when(when)
            def _():
                act(side_copy(s, q, way, target))

    def side_relay(s, q):
        @pl.when(c != s)
        def _():
            side_copy(s, q, 0, ahead).wait_recv()

        side_each(s, q, lambda copy: copy.start())

    def side_source(s):
        @pl.when(c == s)
        def _():
            side[s] = a_ref[0]

    order = (1, 3, 0, 2)

    side_source(0)
    side_source(1)

    @pl.when(r < 2)
    def _():
        panel[core, 0] = a_ref[0]
        panel[core, 1] = a_ref[1]

    for q in order:
        side_relay(0, q)

    @pl.when(r < 2)
    def _():
        for half in range(4):
            wide_start(half)

    @pl.when(r >= 2)
    def _():
        lax.fori_loop(0, 4, lambda half, carry: (wide_relay(half), carry)[1], 0)

    for q in order:
        side_relay(1, q)

    @pl.when(r == 0)
    def _():
        panel[0, 2] = side[1]

    @pl.when(r == 1)
    def _():
        panel[1, 2] = side[0]

    @pl.when(r < 2)
    def _():
        for half in (4, 5):
            wide_start(half)

    @pl.when(r >= 2)
    def _():
        lax.fori_loop(4, 6, lambda half, carry: (wide_relay(half), carry)[1], 0)

    def put(index, value):
        high, low = split(value)
        ph[index] = high
        pl_[index] = low

    def times(i, j):
        return product(ph[i], pl_[i], ph[j], pl_[j])

    @pl.when(r == 0)
    def _():
        pivot[...] = side[0]

    @pl.when(r >= 1)
    def _():
        @pl.when(core == 0)
        def _():
            lax.fori_loop(6, 8, lambda half, carry: (wide_relay(half), carry)[1], 0)

        @pl.when(core == 1)
        def _():
            pair_wait(0, 8)

        put(0, panel[0, 3])
        put(1, panel[0, 2])
        put(2, times(0, 1))
        put(3, side[0])
        reduced = side[1] - times(3, 2)
        pivot[...] = reduced
        put(4, reduced)

    @pl.when(r < 2)
    def _():
        here = lax.broadcasted_iota(jnp.int32, (B, B), 0) == lax.broadcasted_iota(jnp.int32, (B, B), 1)
        block = pivot[...]
        only = jnp.where(here, block, 0.0)
        one_row = 1.0 / jnp.sum(only, axis=0, keepdims=True)
        one_col = 1.0 / jnp.sum(only, axis=1, keepdims=True)
        eye = jnp.where(here, 1.0, 0.0)
        rest = eye - block * one_row
        xf[...] = one_col * (eye + rest)
        high, low = split(rest)
        sh[0, B:] = high
        sl[0, B:] = low
        high, low = split(product(sh[0, B:], sl[0, B:], sh[0, B:], sl[0, B:]))
        sh[1, B:] = high
        sl[1, B:] = low
        high, low = split(xf[...])
        sh[1, :B] = high
        sl[1, :B] = low

        def step(k, carry):
            now = lax.rem(k, 2)
            later = 1 - now
            both = product(sh[now], sl[now], sh[now, B:], sl[now, B:])
            total = xf[...] + both[:B]
            xf[...] = total
            high, low = split(total)
            sh[later, :B] = high
            sl[later, :B] = low
            high, low = split(both[B:])
            sh[later, B:] = high
            sl[later, B:] = low
            return carry

        lax.fori_loop(1, NS_STEPS - 1, step, 0)
        now = (NS_STEPS - 1) % 2
        panel[core, 3] = xf[...] + product(sh[now, :B], sl[now, :B], sh[now, B:], sl[now, B:])
        for half in (6, 7):
            wide_start(half)

    @pl.when(r == 0)
    def _():
        put(0, panel[0, 3])
        for j in range(2):
            put(1, a_ref[j])
            out_ref[j] = times(0, 1)
        pair_wait(0, 8)

    @pl.when(r >= 1)
    def _():
        for j in range(2):
            put(1, panel[0, j])
            put(5 + j, times(0, 1))
            kept = a_ref[j] - times(3, 5 + j)
            out_ref[j] = kept

            @pl.when(r == 1)
            def _():
                put(7 + j, kept)

        @pl.when(r >= 2)
        def _():
            @pl.when(core == 0)
            def _():
                pair_wait(0, 6)

            put(1, panel[1, 2])
            for j in range(2):
                put(7 + j, panel[1, j] - times(1, 5 + j))

            @pl.when(core == 1)
            def _():
                lax.fori_loop(6, 8, lambda half, carry: (wide_relay(half), carry)[1], 0)

            @pl.when(core == 0)
            def _():
                pair_wait(6, 8)

        put(0, panel[1, 3])
        for j in range(2):
            scaled = times(0, 7 + j)
            live = c >= 2 if j == 0 else c >= 0

            @pl.when((r == 1) & live)
            def _():
                out_ref[j] = scaled

            @pl.when((r >= 2) & live)
            def _():
                put(5, scaled)
                out_ref[j] = out_ref[j] - times(4, 5)

    @pl.when(c == 0)
    def _():
        out_ref[0] = a_ref[0]

    def sent(half, carry):
        for tree in range(3):
            each_way(half, tree, lambda copy: copy.wait_send())
        return carry

    lax.fori_loop(0, 8, sent, 0)
    for s in range(2):
        for q in range(4):
            side_each(s, q, lambda copy: copy.wait_send())


def eliminate(blocks):
    vmem = pl.BlockSpec(memory_space=pltpu.VMEM)
    dma = pltpu.SemaphoreType.DMA
    return pl.pallas_call(
        eliminate_kernel,
        out_shape=jax.ShapeDtypeStruct((2, B, B), F32),
        in_specs=[vmem],
        out_specs=vmem,
        scratch_shapes=[
            pltpu.VMEM((2, B, B), F32),
            pltpu.VMEM((2, 4, B, B), F32),
            pltpu.VMEM((B, B), F32),
            pltpu.VMEM((9, B, B), BF16),
            pltpu.VMEM((9, B, B), BF16),
            pltpu.VMEM((2, 2 * B, B), BF16),
            pltpu.VMEM((2, 2 * B, B), BF16),
            pltpu.VMEM((B, B), F32),
            dma((24, 4)),
            dma((24,)),
            dma((24,)),
            dma((2, 4, 3)),
            dma((2, 4)),
        ],
        compiler_params=pltpu.CompilerParams(
            collective_id=1, has_side_effects=True, vmem_limit_bytes=VMEM_LIMIT
        ),
        name="eliminate",
    )(blocks)


def per_device(base, block_mask, heads, coef, weir_node, weir_cell):
    blocks = base.reshape(2, B, B)
    every_head = gather_heads(heads)
    blocks = add_weirs(blocks, block_mask, every_head, coef, weir_node, weir_cell)
    return eliminate(blocks).reshape(base.shape)


def solution(mesh):
    placed = (P(None, "wide", None, "narrow", None, None), P(), P("narrow"), P(), P(), P())
    return jax.shard_map(
        per_device,
        mesh=mesh,
        in_specs=placed,
        out_specs=P(None, "wide", None, "narrow", None, None),
        check_vma=False,
    )
```

```python
import functools

import jax
import jax.numpy as jnp
from jax import lax
from jax.experimental import pallas as pl
from jax.experimental.pallas import tpu as pltpu
from jax.sharding import PartitionSpec as P

NS_STEPS = 6
B = 512
ROWS = 72
LANES = 128
MESH = pl.DeviceIdType.MESH
F32 = jnp.float32
BF16 = jnp.bfloat16
VMEM_LIMIT = 56 * 2**20


def split(x):
    high = x.astype(BF16)
    return high, (x - high.astype(F32)).astype(BF16)


def dot(a, b):
    return jnp.dot(a, b, preferred_element_type=F32)


def dot_nt(a, b):
    return lax.dot_general(a, b, (((1,), (1,)), ((), ())), preferred_element_type=F32)


def product(ah, al, bh, bl):
    return dot(ah, bh) + dot(ah, bl) + dot(al, bh)


def gather_heads_kernel(mine_ref, every_ref, send_sem, recv_sem):
    r = lax.axis_index("wide")
    c = lax.axis_index("narrow")
    count = 8
    barrier = pltpu.get_barrier_semaphore()
    for hop in range(1, count):
        pl.semaphore_signal(barrier, inc=1, device_id=(r, lax.rem(c + hop, count)), device_id_type=MESH)
    pl.semaphore_wait(barrier, count - 1)
    place = pl.ds(pl.multiple_of(c * 8, 8), 8)
    copies = []
    for hop in range(1, count):
        copy = pltpu.make_async_remote_copy(
            src_ref=mine_ref,
            dst_ref=every_ref.at[place],
            send_sem=send_sem.at[hop],
            recv_sem=recv_sem.at[hop],
            device_id=(r, lax.rem(c + hop, count)),
            device_id_type=MESH,
        )
        copy.start()
        copies.append(copy)
    every_ref[place] = mine_ref[...]
    for copy in copies:
        copy.wait()


def gather_heads(heads):
    return pl.pallas_call(
        gather_heads_kernel,
        out_shape=jax.ShapeDtypeStruct((64, LANES), F32),
        in_specs=[pl.BlockSpec(memory_space=pltpu.VMEM)],
        out_specs=pl.BlockSpec(memory_space=pltpu.VMEM),
        scratch_shapes=[pltpu.SemaphoreType.DMA((8,)), pltpu.SemaphoreType.DMA((8,))],
        compiler_params=pltpu.CompilerParams(collective_id=0, has_side_effects=True),
        name="gather_heads",
    )(heads.reshape(8, LANES))


def lookup(table_ref, first, index):
    high = lax.shift_right_logical(index, 7) - first
    low = jnp.bitwise_and(index, 127)
    found = jnp.zeros(index.shape, F32)
    for t in range(32):
        row = jnp.broadcast_to(table_ref[pl.ds(first + t, 1), :], index.shape)
        picked = jnp.take_along_axis(row, low, axis=1, mode="promise_in_bounds")
        found = jnp.where(high == t, picked, found)
    return found


def pieces(x):
    high = x.astype(BF16).astype(F32)
    rest = x - high
    middle = rest.astype(BF16).astype(F32)
    return high, middle, rest - middle


def weirs_kernel(mask_ref, base_ref, heads_ref, coef_ref, node_ref, cell_ref, out_ref, code_ref, flux_ref):
    r = lax.axis_index("wide")
    c = lax.axis_index("narrow")
    upper = r < 8
    for j in range(2):
        col = c + 8 * j
        keep = jnp.where((mask_ref[r, col] != 0) | (r == col), 1.0, 0.0).astype(F32)
        out_ref[j] = base_ref[j] * keep
    node = node_ref[...]
    cell = cell_ref[...]
    drop = lookup(heads_ref, 0, node) - lookup(heads_ref, 32, cell)
    flux = 1.5 * coef_ref[...] * jnp.sqrt(drop * drop + 0.01)
    row = jnp.where(upper, node, cell)
    col = jnp.where(upper, cell, node)
    mine = lax.shift_right_logical(row, 9) == r
    low_row = jnp.bitwise_and(row, 511)

    target = jnp.where(upper, c + 8, c)
    slot = jnp.where(upper, 1, 0)
    hit = jnp.where(mine & (lax.shift_right_logical(col, 9) == target), 1, 0)
    code = low_row * 512 + jnp.bitwise_and(col, 511)
    steps = jnp.max(jnp.sum(hit.astype(F32), axis=0, keepdims=True)).astype(jnp.int32)
    code_ref[...] = jnp.zeros(code_ref.shape, jnp.int32)
    flux_ref[...] = jnp.zeros(flux_ref.shape, F32)
    place = lax.broadcasted_iota(jnp.int32, (ROWS, LANES), 0)

    def extract(s, left):
        first = jnp.min(jnp.where(left != 0, place, ROWS), axis=0, keepdims=True)
        now = place == first
        code_ref[pl.ds(s, 1), :] = jnp.sum(jnp.where(now, code, 0), axis=0, keepdims=True)
        flux_ref[pl.ds(s, 1), :] = jnp.sum(jnp.where(now, flux, 0.0), axis=0, keepdims=True)
        return jnp.where(now, 0, left)

    lax.fori_loop(0, steps, extract, hit)

    def scatter(b, carry):
        rows = pl.ds(pl.multiple_of(b * 8, 8), 8)
        codes = code_ref[rows]
        parts = pieces(flux_ref[rows])
        here = lax.broadcasted_iota(jnp.int32, (B, LANES), 0)
        row_of = lax.shift_right_logical(codes, 9)
        col_of = jnp.bitwise_and(codes, 511)
        right = jnp.concatenate(
            [jnp.where(here == col_of[s : s + 1], 1.0, 0.0).astype(BF16) for s in range(8)], axis=1
        )
        total = jnp.zeros((B, B), F32)
        for part in parts:
            left = jnp.concatenate(
                [jnp.where(here == row_of[s : s + 1], part[s : s + 1], 0.0).astype(BF16) for s in range(8)],
                axis=1,
            )
            total = total + dot_nt(left, right)
        out_ref[slot] = out_ref[slot] - total
        return carry

    lax.fori_loop(0, lax.div(steps + 7, 8), scatter, 0)

    @pl.when(c == lax.rem(r, 8))
    def _():
        own = jnp.where(mine, flux, 0.0)
        parts = pieces(own)
        high = lax.shift_right_logical(low_row, 7)
        low = jnp.bitwise_and(low_row, 127)
        here8 = lax.broadcasted_iota(jnp.int32, (8, LANES), 0)
        here128 = lax.broadcasted_iota(jnp.int32, (LANES, LANES), 0)
        total = jnp.zeros((24, LANES), F32)
        for g in range(ROWS // 8):
            ones = []
            lefts = []
            for s in range(8 * g, 8 * g + 8):
                ones.append(jnp.where(here128 == low[s : s + 1], 1.0, 0.0).astype(BF16))
                at = here8 == high[s : s + 1]
                lefts.append(
                    jnp.concatenate([jnp.where(at, part[s : s + 1], 0.0) for part in parts], axis=0).astype(BF16)
                )
            total = total + dot_nt(jnp.concatenate(lefts, axis=1), jnp.concatenate(ones, axis=1))
        diagonal = total[0:8] + total[8:16] + total[16:24]
        eye = here128 == lax.broadcasted_iota(jnp.int32, (LANES, LANES), 1)
        which = jnp.where(upper, 0, 1)
        for t in range(4):
            part = pl.ds(t * LANES, LANES)
            out_ref[which, part, part] = out_ref[which, part, part] + jnp.where(eye, diagonal[t : t + 1], 0.0)


def add_weirs(base, block_mask, every_head, coef, weir_node, weir_cell):
    pad = ROWS * LANES - coef.shape[0]
    coef = jnp.pad(coef, (0, pad)).reshape(ROWS, LANES)
    node = jnp.pad(weir_node, (0, pad)).reshape(ROWS, LANES)
    cell = jnp.pad(weir_cell, (0, pad), constant_values=4096).reshape(ROWS, LANES)
    vmem = pl.BlockSpec(memory_space=pltpu.VMEM)
    return pl.pallas_call(
        weirs_kernel,
        out_shape=jax.ShapeDtypeStruct((2, B, B), F32),
        in_specs=[pl.BlockSpec(memory_space=pltpu.SMEM)] + [vmem] * 5,
        out_specs=vmem,
        scratch_shapes=[pltpu.VMEM((ROWS, LANES), jnp.int32), pltpu.VMEM((ROWS, LANES), F32)],
        compiler_params=pltpu.CompilerParams(vmem_limit_bytes=VMEM_LIMIT),
        name="add_weirs",
    )(block_mask, base, every_head, coef, node, cell)


def eliminate_kernel(
    a_ref,
    out_ref,
    side,
    row,
    extra,
    pivot,
    ph,
    pl_,
    sh,
    sl,
    xf,
    side_send,
    side_recv,
    row_send,
    row_recv,
    extra_send,
    extra_recv,
    turn,
):
    r = lax.axis_index("wide")
    c = lax.axis_index("narrow")
    core = lax.rem(r, 2)
    chip = lax.div(r, 2)
    pair = (chip * 2 + 1 - core, c)

    barrier = pltpu.get_barrier_semaphore()
    for hop in range(1, 16):
        pl.semaphore_signal(barrier, inc=1, device_id=(lax.rem(r + hop, 16), c), device_id_type=MESH)
    for hop in range(1, 8):
        pl.semaphore_signal(barrier, inc=1, device_id=(r, lax.rem(c + hop, 8)), device_id_type=MESH)
    pl.semaphore_wait(barrier, 22)

    def loop(first, last, act):
        lax.fori_loop(first, last, lambda i, carry: (act(i), carry)[1], 0)

    def side_copy(s, piece, at, target):
        chunk = side.at[s, pl.ds(pl.multiple_of(piece * 64, 64), 64)]
        return pltpu.make_async_remote_copy(
            src_ref=chunk,
            dst_ref=chunk,
            send_sem=side_send.at[s, at],
            recv_sem=side_recv.at[s, piece],
            device_id=(r, target),
            device_id_type=MESH,
        )

    def side_source(s, act):
        def one(hop):
            target = lax.rem(c + hop, 8)
            act(side_copy(s, target, hop, target))
            act(side_copy(s, c, 8 + hop, target))

        @pl.when(c == s)
        def _():
            loop(1, 8, one)

    def side_relay(s, act, wait):
        def one(hop):
            target = lax.rem(c + hop, 8)

            @pl.when(target != s)
            def _():
                act(side_copy(s, c, hop, target))

        @pl.when(c != s)
        def _():
            if wait:
                side_copy(s, c, 0, c).wait_recv()
            loop(1, 8, one)

    def side_wait(s):
        def one(hop):
            piece = lax.rem(c + hop, 8)
            side_copy(s, piece, 0, c).wait_recv()

        @pl.when(c != s)
        def _():
            loop(1, 8, one)

    def row_copy(b, piece, at, target):
        chunk = row.at[b, pl.ds(pl.multiple_of(piece * 32, 32), 32)]
        return pltpu.make_async_remote_copy(
            src_ref=chunk,
            dst_ref=chunk,
            send_sem=row_send.at[b, at],
            recv_sem=row_recv.at[b, piece],
            device_id=(target, c),
            device_id_type=MESH,
        )

    def row_source(b, act):
        def one(t):
            act(row_copy(b, t, t, t))
            act(row_copy(b, lax.rem(t, 2), 16 + t, t))

        loop(2, 16, one)

    def row_pass(b, act, wait):
        def direct(hop):
            target = lax.rem(chip + hop, 8)

            @pl.when(target != 0)
            def _():
                act(row_copy(b, r, hop, target * 2 + core))

        def over(hop):
            piece = lax.rem(chip + hop, 8) * 2 + core
            if wait:
                row_copy(b, piece, 0, r).wait_recv()
            act(row_copy(b, piece, 8 + hop, pair[0]))

        if wait:
            row_copy(b, r, 0, r).wait_recv()
        loop(1, 8, direct)
        act(row_copy(b, r, 8, pair[0]))
        loop(1, 8, over)

    def row_wait(b):
        def one(q):
            row_copy(b, q * 2 + 1 - core, 0, r).wait_recv()

        loop(0, 8, one)

    def extra_copy(src, at):
        return pltpu.make_async_remote_copy(
            src_ref=src,
            dst_ref=extra.at[at],
            send_sem=extra_send.at[at],
            recv_sem=extra_recv.at[at],
            device_id=pair,
            device_id_type=MESH,
        )

    start = lambda copy: copy.start()
    sent = lambda copy: copy.wait_send()

    def put(index, value):
        high, low = split(value)
        ph[index] = high
        pl_[index] = low

    def times(i, j):
        return product(ph[i], pl_[i], ph[j], pl_[j])

    def invert():
        here = lax.broadcasted_iota(jnp.int32, (B, B), 0) == lax.broadcasted_iota(jnp.int32, (B, B), 1)
        block = pivot[...]
        only = jnp.where(here, block, 0.0)
        one_row = 1.0 / jnp.sum(only, axis=0, keepdims=True)
        one_col = 1.0 / jnp.sum(only, axis=1, keepdims=True)
        eye = jnp.where(here, 1.0, 0.0)
        rest = eye - block * one_row
        xf[...] = one_col * (eye + rest)
        high, low = split(rest)
        sh[0, B:] = high
        sl[0, B:] = low
        high, low = split(product(sh[0, B:], sl[0, B:], sh[0, B:], sl[0, B:]))
        sh[1, B:] = high
        sl[1, B:] = low
        high, low = split(xf[...])
        sh[1, :B] = high
        sl[1, :B] = low

        def step(k):
            now = lax.rem(k, 2)
            later = 1 - now
            both = product(sh[now], sl[now], sh[now, B:], sl[now, B:])
            total = xf[...] + both[:B]
            xf[...] = total
            high, low = split(total)
            sh[later, :B] = high
            sl[later, :B] = low
            high, low = split(both[B:])
            sh[later, B:] = high
            sl[later, B:] = low

        loop(1, NS_STEPS - 1, step)
        now = (NS_STEPS - 1) % 2
        return xf[...] + product(sh[now, :B], sl[now, :B], sh[now, B:], sl[now, B:])

    @pl.when(c == 0)
    def _():
        side[0] = a_ref[0]

    @pl.when((c == 1) & (r < 2))
    def _():
        side[1] = a_ref[0]

    @pl.when(r == 1)
    def _():
        pl.semaphore_wait(turn, 1)

    side_source(0, start)
    side_relay(0, start, True)
    side_wait(0)

    @pl.when(r == 0)
    def _():
        pl.semaphore_signal(turn, inc=1, device_id=pair, device_id_type=MESH)

    @pl.when(r < 2)
    def _():
        side_source(1, start)

    @pl.when(r == 0)
    def _():
        extra_copy(a_ref.at[0], 1).start()
        extra_copy(a_ref.at[1], 2).start()
        pivot[...] = side[0]
        xf_first = invert()
        xf[...] = xf_first
        extra_copy(xf, 0).start()
        put(0, xf_first)
        side_relay(1, start, True)
        side_wait(1)
        put(1, side[1])
        put(2, times(0, 1))
        for at in (0, 1):
            extra_copy(extra.at[at], at).wait_recv()
        put(3, extra[0])
        pivot[...] = extra[1] - times(3, 2)
        extra_copy(xf, 0).wait_send()
        row[4] = invert()
        row_source(4, start)
        extra_copy(row.at[4], 3).start()
        for j in range(2):
            put(1, a_ref[j])
            out_ref[j] = times(0, 1)
        row_source(4, sent)
        for at in (1, 2):
            extra_copy(a_ref.at[at - 1], at).wait_send()

    @pl.when(r == 1)
    def _():
        extra_copy(side.at[0], 0).start()
        side_relay(1, start, True)
        side_wait(1)
        extra_copy(side.at[1], 1).start()
        for at in range(3):
            extra_copy(extra.at[at], at).wait_recv()
        put(0, extra[0])
        put(3, side[0])
        for j in range(2):
            put(1, extra[1 + j])
            scaled = times(0, 1)
            row[j] = scaled
            row_source(j, start)
            put(4 + j, scaled)
        for j in range(2):
            kept = a_ref[j] - times(3, 4 + j)
            row[2 + j] = kept
            row_source(2 + j, start)
            out_ref[j] = kept
            put(6 + j, kept)

    @pl.when(r >= 2)
    def _():
        put(3, side[0])
        for j in range(2):
            row_pass(j, start, True)
        for j in range(2):
            row_wait(j)
            put(4 + j, row[j])
            kept = a_ref[j] - times(3, 4 + j)
            out_ref[j] = kept
            if j == 0:

                @pl.when(c == 1)
                def _():
                    side[1] = kept

                side_source(1, start)
        for j in range(2):
            row_pass(2 + j, start, True)
        side_relay(1, start, True)
        for j in range(2):
            row_wait(2 + j)
            put(6 + j, row[2 + j])
        side_wait(1)
        put(4, side[1])
        row_pass(4, start, True)
        row_wait(4)

    @pl.when(r == 1)
    def _():
        extra_copy(row.at[4], 3).wait_recv()
        put(0, extra[3])

    @pl.when(r >= 2)
    def _():
        put(0, row[4])

    @pl.when(r >= 1)
    def _():
        for j in range(2):
            scaled = times(0, 6 + j)
            live = c >= 2 if j == 0 else c >= 0

            @pl.when((r == 1) & live)
            def _():
                out_ref[j] = scaled

            @pl.when((r >= 2) & live)
            def _():
                put(5, scaled)
                out_ref[j] = out_ref[j] - times(4, 5)

    @pl.when(c == 0)
    def _():
        out_ref[0] = a_ref[0]

    for s in range(2):
        side_source(s, sent)
        side_relay(s, sent, False)

    @pl.when(r == 0)
    def _():
        extra_copy(row.at[4], 3).wait_send()

    @pl.when(r == 1)
    def _():
        for at in (0, 1):
            extra_copy(side.at[at], at).wait_send()
        for b in range(4):
            row_source(b, sent)

    @pl.when(r >= 2)
    def _():
        loop(0, 5, lambda b: row_pass(b, sent, False))


def eliminate(blocks):
    vmem = pl.BlockSpec(memory_space=pltpu.VMEM)
    dma = pltpu.SemaphoreType.DMA
    return pl.pallas_call(
        eliminate_kernel,
        out_shape=jax.ShapeDtypeStruct((2, B, B), F32),
        in_specs=[vmem],
        out_specs=vmem,
        scratch_shapes=[
            pltpu.VMEM((2, B, B), F32),
            pltpu.VMEM((5, B, B), F32),
            pltpu.VMEM((4, B, B), F32),
            pltpu.VMEM((B, B), F32),
            pltpu.VMEM((8, B, B), BF16),
            pltpu.VMEM((8, B, B), BF16),
            pltpu.VMEM((2, 2 * B, B), BF16),
            pltpu.VMEM((2, 2 * B, B), BF16),
            pltpu.VMEM((B, B), F32),
            dma((2, 16)),
            dma((2, 8)),
            dma((5, 32)),
            dma((5, 16)),
            dma((4,)),
            dma((4,)),
            pltpu.SemaphoreType.REGULAR,
        ],
        compiler_params=pltpu.CompilerParams(
            collective_id=1, has_side_effects=True, vmem_limit_bytes=VMEM_LIMIT
        ),
        name="eliminate",
    )(blocks)


def per_device(base, block_mask, heads, coef, weir_node, weir_cell):
    blocks = base.reshape(2, B, B)
    every_head = gather_heads(heads)
    blocks = add_weirs(blocks, block_mask, every_head, coef, weir_node, weir_cell)
    return eliminate(blocks).reshape(base.shape)


def solution(mesh):
    placed = (P(None, "wide", None, "narrow", None, None), P(), P("narrow"), P(), P(), P())
    return jax.shard_map(
        per_device,
        mesh=mesh,
        in_specs=placed,
        out_specs=P(None, "wide", None, "narrow", None, None),
        check_vma=False,
    )
```

```python
import functools

import jax
import jax.numpy as jnp
from jax import lax
from jax.experimental import pallas as pl
from jax.experimental.pallas import tpu as pltpu
from jax.sharding import PartitionSpec as P

NS_STEPS = 6
B = 512
ROWS = 72
LANES = 128
MESH = pl.DeviceIdType.MESH
F32 = jnp.float32
BF16 = jnp.bfloat16
VMEM_LIMIT = 56 * 2**20
SLOTS = 2
WIDE_DEPTH = ((0, 1, 2, 3, 3, 2, 3, 4), (0, 3, 2, 1, 3, 4, 3, 2), (0, 3, 4, 3, 1, 2, 3, 2))
WIDE_WAYS = (
    ((1, 1, 1, 0, 0, 0, 1, 0), (0, 0, 0, 0, 0, 1, 0, 0), (0, 1, 1, 0, 0, 0, 0, 0)),
    ((0, 0, 0, 0, 0, 0, 0, 1), (1, 0, 1, 1, 0, 0, 1, 1), (0, 0, 0, 1, 0, 0, 0, 0)),
    ((0, 0, 0, 0, 1, 1, 0, 0), (0, 0, 0, 0, 1, 0, 0, 0), (1, 0, 0, 0, 0, 1, 1, 1)),
)
SIDE_DEPTH = ((0, 1, 2, 3, 1, 2, 3, 2), (0, 1, 2, 3, 3, 2, 3, 4), (0, 3, 2, 1, 5, 4, 3, 4), (0, 3, 2, 1, 3, 4, 3, 2))
SIDE_WAYS = (
    ((1, 1, 1, 0, 1, 1, 0, 0), (0, 0, 0, 0, 1, 0, 0, 0), (1, 0, 0, 0, 0, 0, 0, 0)),
    ((1, 1, 1, 0, 0, 1, 0, 0), (0, 0, 0, 0, 1, 1, 0, 0), (0, 1, 0, 0, 0, 0, 0, 0)),
    ((0, 0, 0, 0, 0, 0, 1, 1), (1, 0, 1, 1, 0, 0, 1, 0), (0, 0, 1, 0, 0, 0, 0, 0)),
    ((0, 0, 0, 0, 0, 0, 0, 1), (1, 0, 1, 1, 0, 0, 1, 1), (0, 0, 0, 1, 0, 0, 0, 0)),
)


def split(x):
    high = x.astype(BF16)
    return high, (x - high.astype(F32)).astype(BF16)


def dot(a, b):
    return jnp.dot(a, b, preferred_element_type=F32)


def dot_nt(a, b):
    return lax.dot_general(a, b, (((1,), (1,)), ((), ())), preferred_element_type=F32)


def product(ah, al, bh, bl):
    return dot(ah, bh) + dot(ah, bl) + dot(al, bh)


def gather_heads_kernel(mine_ref, every_ref, send_sem, recv_sem):
    r = lax.axis_index("wide")
    c = lax.axis_index("narrow")
    count = 8
    barrier = pltpu.get_barrier_semaphore()
    for hop in range(1, count):
        pl.semaphore_signal(barrier, inc=1, device_id=(r, lax.rem(c + hop, count)), device_id_type=MESH)
    pl.semaphore_wait(barrier, count - 1)
    place = pl.ds(pl.multiple_of(c * 8, 8), 8)
    copies = []
    for hop in range(1, count):
        copy = pltpu.make_async_remote_copy(
            src_ref=mine_ref,
            dst_ref=every_ref.at[place],
            send_sem=send_sem.at[hop],
            recv_sem=recv_sem.at[hop],
            device_id=(r, lax.rem(c + hop, count)),
            device_id_type=MESH,
        )
        copy.start()
        copies.append(copy)
    every_ref[place] = mine_ref[...]
    for copy in copies:
        copy.wait()


def gather_heads(heads):
    return pl.pallas_call(
        gather_heads_kernel,
        out_shape=jax.ShapeDtypeStruct((64, LANES), F32),
        in_specs=[pl.BlockSpec(memory_space=pltpu.VMEM)],
        out_specs=pl.BlockSpec(memory_space=pltpu.VMEM),
        scratch_shapes=[pltpu.SemaphoreType.DMA((8,)), pltpu.SemaphoreType.DMA((8,))],
        compiler_params=pltpu.CompilerParams(collective_id=0, has_side_effects=True),
        name="gather_heads",
    )(heads.reshape(8, LANES))


def lookup(table_ref, first, index):
    high = lax.shift_right_logical(index, 7) - first
    low = jnp.bitwise_and(index, 127)
    found = jnp.zeros(index.shape, F32)
    for t in range(32):
        row = jnp.broadcast_to(table_ref[pl.ds(first + t, 1), :], index.shape)
        picked = jnp.take_along_axis(row, low, axis=1, mode="promise_in_bounds")
        found = jnp.where(high == t, picked, found)
    return found


def pieces(x):
    high = x.astype(BF16).astype(F32)
    rest = x - high
    middle = rest.astype(BF16).astype(F32)
    return high, middle, rest - middle


def weirs_kernel(mask_ref, base_ref, heads_ref, coef_ref, node_ref, cell_ref, out_ref, code_ref, flux_ref):
    r = lax.axis_index("wide")
    c = lax.axis_index("narrow")
    upper = r < 8
    for j in range(2):
        col = c + 8 * j
        keep = jnp.where((mask_ref[r, col] != 0) | (r == col), 1.0, 0.0).astype(F32)
        out_ref[j] = base_ref[j] * keep
    node = node_ref[...]
    cell = cell_ref[...]
    drop = lookup(heads_ref, 0, node) - lookup(heads_ref, 32, cell)
    flux = 1.5 * coef_ref[...] * jnp.sqrt(drop * drop + 0.01)
    row = jnp.where(upper, node, cell)
    col = jnp.where(upper, cell, node)
    mine = lax.shift_right_logical(row, 9) == r
    low_row = jnp.bitwise_and(row, 511)

    target = jnp.where(upper, c + 8, c)
    slot = jnp.where(upper, 1, 0)
    hit = jnp.where(mine & (lax.shift_right_logical(col, 9) == target), 1, 0)
    code = low_row * 512 + jnp.bitwise_and(col, 511)
    steps = jnp.max(jnp.sum(hit.astype(F32), axis=0, keepdims=True)).astype(jnp.int32)
    code_ref[...] = jnp.zeros(code_ref.shape, jnp.int32)
    flux_ref[...] = jnp.zeros(flux_ref.shape, F32)
    place = lax.broadcasted_iota(jnp.int32, (ROWS, LANES), 0)

    def extract(s, left):
        first = jnp.min(jnp.where(left != 0, place, ROWS), axis=0, keepdims=True)
        now = place == first
        code_ref[pl.ds(s, 1), :] = jnp.sum(jnp.where(now, code, 0), axis=0, keepdims=True)
        flux_ref[pl.ds(s, 1), :] = jnp.sum(jnp.where(now, flux, 0.0), axis=0, keepdims=True)
        return jnp.where(now, 0, left)

    lax.fori_loop(0, steps, extract, hit)

    def scatter(b, carry):
        rows = pl.ds(pl.multiple_of(b * 8, 8), 8)
        codes = code_ref[rows]
        parts = pieces(flux_ref[rows])
        here = lax.broadcasted_iota(jnp.int32, (B, LANES), 0)
        row_of = lax.shift_right_logical(codes, 9)
        col_of = jnp.bitwise_and(codes, 511)
        right = jnp.concatenate(
            [jnp.where(here == col_of[s : s + 1], 1.0, 0.0).astype(BF16) for s in range(8)], axis=1
        )
        total = jnp.zeros((B, B), F32)
        for part in parts:
            left = jnp.concatenate(
                [jnp.where(here == row_of[s : s + 1], part[s : s + 1], 0.0).astype(BF16) for s in range(8)],
                axis=1,
            )
            total = total + dot_nt(left, right)
        out_ref[slot] = out_ref[slot] - total
        return carry

    lax.fori_loop(0, lax.div(steps + 7, 8), scatter, 0)

    @pl.when(c == lax.rem(r, 8))
    def _():
        own = jnp.where(mine, flux, 0.0)
        parts = pieces(own)
        high = lax.shift_right_logical(low_row, 7)
        low = jnp.bitwise_and(low_row, 127)
        here8 = lax.broadcasted_iota(jnp.int32, (8, LANES), 0)
        here128 = lax.broadcasted_iota(jnp.int32, (LANES, LANES), 0)
        total = jnp.zeros((24, LANES), F32)
        for g in range(ROWS // 8):
            ones = []
            lefts = []
            for s in range(8 * g, 8 * g + 8):
                ones.append(jnp.where(here128 == low[s : s + 1], 1.0, 0.0).astype(BF16))
                at = here8 == high[s : s + 1]
                lefts.append(
                    jnp.concatenate([jnp.where(at, part[s : s + 1], 0.0) for part in parts], axis=0).astype(BF16)
                )
            total = total + dot_nt(jnp.concatenate(lefts, axis=1), jnp.concatenate(ones, axis=1))
        diagonal = total[0:8] + total[8:16] + total[16:24]
        eye = here128 == lax.broadcasted_iota(jnp.int32, (LANES, LANES), 1)
        which = jnp.where(upper, 0, 1)
        for t in range(4):
            part = pl.ds(t * LANES, LANES)
            out_ref[which, part, part] = out_ref[which, part, part] + jnp.where(eye, diagonal[t : t + 1], 0.0)


def add_weirs(base, block_mask, every_head, coef, weir_node, weir_cell):
    pad = ROWS * LANES - coef.shape[0]
    coef = jnp.pad(coef, (0, pad)).reshape(ROWS, LANES)
    node = jnp.pad(weir_node, (0, pad)).reshape(ROWS, LANES)
    cell = jnp.pad(weir_cell, (0, pad), constant_values=4096).reshape(ROWS, LANES)
    vmem = pl.BlockSpec(memory_space=pltpu.VMEM)
    return pl.pallas_call(
        weirs_kernel,
        out_shape=jax.ShapeDtypeStruct((2, B, B), F32),
        in_specs=[pl.BlockSpec(memory_space=pltpu.SMEM)] + [vmem] * 5,
        out_specs=vmem,
        scratch_shapes=[pltpu.VMEM((ROWS, LANES), jnp.int32), pltpu.VMEM((ROWS, LANES), F32)],
        compiler_params=pltpu.CompilerParams(vmem_limit_bytes=VMEM_LIMIT),
        name="add_weirs",
    )(block_mask, base, every_head, coef, node, cell)


def eliminate_kernel(
    a_ref,
    out_ref,
    side,
    panel,
    last,
    pivot,
    ph,
    pl_,
    sh,
    sl,
    xf,
    wide_send,
    wide_recv,
    pair_send,
    pair_recv,
    side_send,
    side_recv,
    last_sem,
):
    r = lax.axis_index("wide")
    c = lax.axis_index("narrow")
    core = lax.rem(r, 2)
    chip = lax.div(r, 2)
    y = lax.rem(chip, 4)
    x = lax.div(chip, 4)
    z = lax.rem(c, 4)
    far = lax.div(c, 4)
    up = (x * 8 + lax.rem(y + 1, 4) * 2 + core, c)
    down = (x * 8 + lax.rem(y + 3, 4) * 2 + core, c)
    across = ((1 - x) * 8 + y * 2 + core, c)
    pair = (chip * 2 + 1 - core, c)
    ahead = (r, far * 4 + lax.rem(z + 1, 4))
    behind = (r, far * 4 + lax.rem(z + 3, 4))
    over = (r, (1 - far) * 4 + z)

    barrier = pltpu.get_barrier_semaphore()
    for peer in (up, down, across, pair, ahead, behind, over):
        pl.semaphore_signal(barrier, inc=1, device_id=peer, device_id_type=MESH)
    pl.semaphore_wait(barrier, 7)

    def loop(first, last, act):
        lax.fori_loop(first, last, lambda i, carry: (act(i), carry)[1], 0)

    def pick(values, at):
        return sum(jnp.where(at == i, v, 0) for i, v in enumerate(values) if v)

    start = lambda copy: copy.start()
    sent = lambda copy: copy.wait_send()

    depth = tuple(pick(values, chip) for values in WIDE_DEPTH)
    ways = tuple(tuple(pick(values, chip) == 1 for values in tree) for tree in WIDE_WAYS)

    def wide_copy(j, way, target):
        rows = pl.ds(pl.multiple_of(lax.rem(j, 8) * 64, 64), 64)
        chunk = panel.at[core, lax.div(j, 8), rows]
        return pltpu.make_async_remote_copy(
            src_ref=chunk,
            dst_ref=chunk,
            send_sem=wide_send.at[j, way],
            recv_sem=wide_recv.at[j],
            device_id=target,
            device_id_type=MESH,
        )

    def wide_each(tree, j, act):
        for way, target in enumerate((up, down, across)):

            @pl.when(ways[tree][way])
            def _():
                act(wide_copy(j, way, target))

    def wide_slot(first, end, slot):
        for tree in range(3):
            j = 3 * (slot - SLOTS * depth[tree]) + tree

            @pl.when((j >= first) & (j < end))
            def _():
                wide_copy(j, 0, up).wait_recv()
                wide_each(tree, j, start)

    def wide_relay(first, end):
        loop(first // 3 - 1, (end + 2) // 3 + 4 * SLOTS, lambda slot: wide_slot(first, end, slot))

    def wide_source(first, end, act):
        def one(j):
            for tree in range(3):

                @pl.when(lax.rem(j, 3) == tree)
                def _():
                    wide_each(tree, j, act)

        loop(first, end, one)

    def pair_copy(b):
        block = panel.at[core, b]
        return pltpu.make_async_remote_copy(
            src_ref=block,
            dst_ref=block,
            send_sem=pair_send.at[b],
            recv_sem=pair_recv.at[b],
            device_id=pair,
            device_id_type=MESH,
        )

    def pair_wait(b):
        block = panel.at[1 - core, b]
        pltpu.make_async_remote_copy(
            src_ref=block,
            dst_ref=block,
            send_sem=pair_send.at[b],
            recv_sem=pair_recv.at[b],
            device_id=pair,
            device_id_type=MESH,
        ).wait_recv()

    def side_copy(s, q, u, way, target):
        chunk = side.at[s, pl.ds(pl.multiple_of(q * 128 + u * 64, 64), 64)]
        return pltpu.make_async_remote_copy(
            src_ref=chunk,
            dst_ref=chunk,
            send_sem=side_send.at[s, q, u, way],
            recv_sem=side_recv.at[s, q, u],
            device_id=target,
            device_id_type=MESH,
        )

    def side_each(s, q, u, act):
        place = far * 4 + lax.rem(z + 4 - s, 4)
        for way, target in enumerate((ahead, behind, over)):

            @pl.when(pick(SIDE_WAYS[q][way], place) == 1)
            def _():
                act(side_copy(s, q, u, way, target))

    def side_slot(slot):
        for s in range(2):
            place = far * 4 + lax.rem(z + 4 - s, 4)
            for q in (1, 3, 0, 2):
                at = slot - 4 * s - (1 if q % 2 == 0 else 0) - SLOTS * pick(SIDE_DEPTH[q], place)

                @pl.when((at == 0) | (at == 2))
                def _():
                    u = lax.div(at, 2)

                    @pl.when(c != s)
                    def _():
                        side_copy(s, q, u, 0, ahead).wait_recv()

                    side_each(s, q, u, start)

    SIDE_END = 8 + 5 * SLOTS

    def put(index, value):
        high, low = split(value)
        ph[index] = high
        pl_[index] = low

    def times(i, j):
        return product(ph[i], pl_[i], ph[j], pl_[j])

    def invert(hook):
        here = lax.broadcasted_iota(jnp.int32, (B, B), 0) == lax.broadcasted_iota(jnp.int32, (B, B), 1)
        block = pivot[...]
        only = jnp.where(here, block, 0.0)
        one_row = 1.0 / jnp.sum(only, axis=0, keepdims=True)
        one_col = 1.0 / jnp.sum(only, axis=1, keepdims=True)
        eye = jnp.where(here, 1.0, 0.0)
        rest = eye - block * one_row
        xf[...] = one_col * (eye + rest)
        high, low = split(rest)
        sh[0, B:] = high
        sl[0, B:] = low
        high, low = split(product(sh[0, B:], sl[0, B:], sh[0, B:], sl[0, B:]))
        sh[1, B:] = high
        sl[1, B:] = low
        high, low = split(xf[...])
        sh[1, :B] = high
        sl[1, :B] = low

        def step(k):
            now = lax.rem(k, 2)
            later = 1 - now
            both = product(sh[now], sl[now], sh[now, B:], sl[now, B:])
            total = xf[...] + both[:B]
            xf[...] = total
            high, low = split(total)
            sh[later, :B] = high
            sl[later, :B] = low
            high, low = split(both[B:])
            sh[later, B:] = high
            sl[later, B:] = low
            hook(k)

        loop(1, NS_STEPS - 1, step)
        now = (NS_STEPS - 1) % 2
        return xf[...] + product(sh[now, :B], sl[now, :B], sh[now, B:], sl[now, B:])

    last_copy = pltpu.make_async_remote_copy(
        src_ref=side.at[1],
        dst_ref=last,
        send_sem=last_sem.at[0],
        recv_sem=last_sem.at[1],
        device_id=pair,
        device_id_type=MESH,
    )

    for s in range(2):

        @pl.when(c == s)
        def _():
            side[s] = a_ref[0]

    @pl.when(r < 2)
    def _():
        panel[core, 0] = a_ref[0]
        panel[core, 1] = a_ref[1]
        wide_source(0, 16, start)
        pair_copy(0).start()
        pair_copy(1).start()

    @pl.when(r == 0)
    def _():
        loop(0, SIDE_END - 4, side_slot)
        pivot[...] = side[0]
        first = invert(lambda k: side_slot(SIDE_END - 5 + k))
        panel[0, 3] = first
        wide_source(24, 32, start)
        pair_copy(3).start()
        panel[0, 2] = side[1]
        wide_source(16, 24, start)
        pair_copy(2).start()
        put(0, first)
        put(1, side[1])
        put(2, times(0, 1))
        pair_wait(2)
        put(3, panel[1, 2])
        last_copy.wait_recv()
        pivot[...] = last[...] - times(3, 2)
        panel[0, 4] = invert(lambda k: None)
        wide_source(32, 40, start)
        pair_copy(4).start()
        for j in range(2):
            put(1, a_ref[j])
            out_ref[j] = times(0, 1)
        pair_wait(0)
        pair_wait(1)

    @pl.when(r == 1)
    def _():
        loop(0, SIDE_END, side_slot)
        panel[1, 2] = side[0]
        last_copy.start()
        pair_copy(2).start()
        wide_source(16, 24, start)

    @pl.when(r >= 2)
    def _():
        def early(slot):
            side_slot(slot)
            wide_slot(0, 16, slot)

        loop(0, max(SIDE_END, 6 + 4 * SLOTS), early)
        pair_copy(0).start()
        pair_copy(1).start()

    @pl.when((r >= 2) & (core == 0))
    def _():
        wide_relay(24, 32)
        pair_copy(3).start()
        wide_relay(16, 24)
        pair_copy(2).start()
        pair_wait(0)
        pair_wait(1)
        pair_wait(2)

    @pl.when((r >= 2) & (core == 1))
    def _():
        wide_relay(16, 24)
        pair_copy(2).start()

    @pl.when(core == 1)
    def _():
        for b in range(4):
            pair_wait(b)

    @pl.when(r >= 1)
    def _():
        put(0, panel[0, 3])
        put(3, side[0])
        for j in range(2):
            put(1, panel[0, j])
            put(4 + j, times(0, 1))
            kept = a_ref[j] - times(3, 4 + j)
            out_ref[j] = kept

            @pl.when(r == 1)
            def _():
                put(6 + j, kept)

        @pl.when(r >= 2)
        def _():
            put(1, panel[1, 2])
            for j in range(2):
                put(6 + j, panel[1, j] - times(1, 4 + j))
            put(1, panel[0, 2])
            put(2, times(0, 1))
            put(4, side[1] - times(3, 2))

        @pl.when((r >= 2) & (core == 0))
        def _():
            wide_relay(32, 40)
            pair_copy(4).start()

        @pl.when(core == 1)
        def _():
            pair_wait(4)

        put(0, panel[0, 4])
        for j in range(2):
            scaled = times(0, 6 + j)
            live = c >= 2 if j == 0 else c >= 0

            @pl.when((r == 1) & live)
            def _():
                out_ref[j] = scaled

            @pl.when((r >= 2) & live)
            def _():
                put(5, scaled)
                out_ref[j] = out_ref[j] - times(4, 5)

    @pl.when(c == 0)
    def _():
        out_ref[0] = a_ref[0]

    for s in range(2):
        for q in range(4):
            for u in range(2):
                side_each(s, q, u, sent)

    @pl.when(core == 0)
    def _():
        wide_source(0, 40, sent)
        for b in range(5):
            pair_copy(b).wait_send()

    @pl.when(core == 1)
    def _():
        wide_source(0, 24, sent)
        for b in range(3):
            pair_copy(b).wait_send()

    @pl.when(r == 1)
    def _():
        last_copy.wait_send()


def eliminate(blocks):
    vmem = pl.BlockSpec(memory_space=pltpu.VMEM)
    dma = pltpu.SemaphoreType.DMA
    return pl.pallas_call(
        eliminate_kernel,
        out_shape=jax.ShapeDtypeStruct((2, B, B), F32),
        in_specs=[vmem],
        out_specs=vmem,
        scratch_shapes=[
            pltpu.VMEM((2, B, B), F32),
            pltpu.VMEM((2, 5, B, B), F32),
            pltpu.VMEM((B, B), F32),
            pltpu.VMEM((B, B), F32),
            pltpu.VMEM((8, B, B), BF16),
            pltpu.VMEM((8, B, B), BF16),
            pltpu.VMEM((2, 2 * B, B), BF16),
            pltpu.VMEM((2, 2 * B, B), BF16),
            pltpu.VMEM((B, B), F32),
            dma((40, 3)),
            dma((40,)),
            dma((5,)),
            dma((5,)),
            dma((2, 4, 2, 3)),
            dma((2, 4, 2)),
            dma((2,)),
        ],
        compiler_params=pltpu.CompilerParams(
            collective_id=1, has_side_effects=True, vmem_limit_bytes=VMEM_LIMIT
        ),
        name="eliminate",
    )(blocks)


def per_device(base, block_mask, heads, coef, weir_node, weir_cell):
    blocks = base.reshape(2, B, B)
    every_head = gather_heads(heads)
    blocks = add_weirs(blocks, block_mask, every_head, coef, weir_node, weir_cell)
    return eliminate(blocks).reshape(base.shape)


def solution(mesh):
    placed = (P(None, "wide", None, "narrow", None, None), P(), P("narrow"), P(), P(), P())
    return jax.shard_map(
        per_device,
        mesh=mesh,
        in_specs=placed,
        out_specs=P(None, "wide", None, "narrow", None, None),
        check_vma=False,
    )
```

```python
import functools

import jax
import jax.numpy as jnp
from jax import lax
from jax.experimental import pallas as pl
from jax.experimental.pallas import tpu as pltpu
from jax.sharding import PartitionSpec as P

NS_STEPS = 6
B = 512
ROWS = 72
LANES = 128
MESH = pl.DeviceIdType.MESH
F32 = jnp.float32
BF16 = jnp.bfloat16
VMEM_LIMIT = 56 * 2**20
SLOTS = 2
CHUNK = 32
PARTS = B // CHUNK
TREE_DEPTH = ((0, 1, 2, 3, 3, 2, 3, 4), (0, 3, 2, 1, 3, 4, 3, 2), (0, 3, 4, 3, 1, 2, 3, 2))
TREE_WAYS = (
    ((1, 1, 1, 0, 0, 0, 1, 0), (0, 0, 0, 0, 0, 1, 0, 0), (0, 1, 1, 0, 0, 0, 0, 0)),
    ((0, 0, 0, 0, 0, 0, 0, 1), (1, 0, 1, 1, 0, 0, 1, 1), (0, 0, 0, 1, 0, 0, 0, 0)),
    ((0, 0, 0, 0, 1, 1, 0, 0), (0, 0, 0, 0, 1, 0, 0, 0), (1, 0, 0, 0, 0, 1, 1, 1)),
)


def split(x):
    high = x.astype(BF16)
    return high, (x - high.astype(F32)).astype(BF16)


def dot(a, b):
    return jnp.dot(a, b, preferred_element_type=F32)


def dot_nt(a, b):
    return lax.dot_general(a, b, (((1,), (1,)), ((), ())), preferred_element_type=F32)


def product(ah, al, bh, bl):
    return dot(ah, bh) + dot(ah, bl) + dot(al, bh)


def gather_heads_kernel(mine_ref, every_ref, send_sem, recv_sem):
    r = lax.axis_index("wide")
    c = lax.axis_index("narrow")
    count = 8
    barrier = pltpu.get_barrier_semaphore()
    for hop in range(1, count):
        pl.semaphore_signal(barrier, inc=1, device_id=(r, lax.rem(c + hop, count)), device_id_type=MESH)
    pl.semaphore_wait(barrier, count - 1)
    place = pl.ds(pl.multiple_of(c * 8, 8), 8)
    copies = []
    for hop in range(1, count):
        copy = pltpu.make_async_remote_copy(
            src_ref=mine_ref,
            dst_ref=every_ref.at[place],
            send_sem=send_sem.at[hop],
            recv_sem=recv_sem.at[hop],
            device_id=(r, lax.rem(c + hop, count)),
            device_id_type=MESH,
        )
        copy.start()
        copies.append(copy)
    every_ref[place] = mine_ref[...]
    for copy in copies:
        copy.wait()


def gather_heads(heads):
    return pl.pallas_call(
        gather_heads_kernel,
        out_shape=jax.ShapeDtypeStruct((64, LANES), F32),
        in_specs=[pl.BlockSpec(memory_space=pltpu.VMEM)],
        out_specs=pl.BlockSpec(memory_space=pltpu.VMEM),
        scratch_shapes=[pltpu.SemaphoreType.DMA((8,)), pltpu.SemaphoreType.DMA((8,))],
        compiler_params=pltpu.CompilerParams(collective_id=0, has_side_effects=True),
        name="gather_heads",
    )(heads.reshape(8, LANES))


def lookup(table_ref, first, index):
    high = lax.shift_right_logical(index, 7) - first
    low = jnp.bitwise_and(index, 127)
    found = jnp.zeros(index.shape, F32)
    for t in range(32):
        row = jnp.broadcast_to(table_ref[pl.ds(first + t, 1), :], index.shape)
        picked = jnp.take_along_axis(row, low, axis=1, mode="promise_in_bounds")
        found = jnp.where(high == t, picked, found)
    return found


def pieces(x):
    high = x.astype(BF16).astype(F32)
    rest = x - high
    middle = rest.astype(BF16).astype(F32)
    return high, middle, rest - middle


def weirs_kernel(mask_ref, base_ref, heads_ref, coef_ref, node_ref, cell_ref, out_ref, code_ref, flux_ref):
    r = lax.axis_index("wide")
    c = lax.axis_index("narrow")
    upper = r < 8
    for j in range(2):
        col = c + 8 * j
        keep = jnp.where((mask_ref[r, col] != 0) | (r == col), 1.0, 0.0).astype(F32)
        out_ref[j] = base_ref[j] * keep
    node = node_ref[...]
    cell = cell_ref[...]
    drop = lookup(heads_ref, 0, node) - lookup(heads_ref, 32, cell)
    flux = 1.5 * coef_ref[...] * jnp.sqrt(drop * drop + 0.01)
    row = jnp.where(upper, node, cell)
    col = jnp.where(upper, cell, node)
    mine = lax.shift_right_logical(row, 9) == r
    low_row = jnp.bitwise_and(row, 511)

    target = jnp.where(upper, c + 8, c)
    slot = jnp.where(upper, 1, 0)
    hit = jnp.where(mine & (lax.shift_right_logical(col, 9) == target), 1, 0)
    code = low_row * 512 + jnp.bitwise_and(col, 511)
    steps = jnp.max(jnp.sum(hit.astype(F32), axis=0, keepdims=True)).astype(jnp.int32)
    code_ref[...] = jnp.zeros(code_ref.shape, jnp.int32)
    flux_ref[...] = jnp.zeros(flux_ref.shape, F32)
    place = lax.broadcasted_iota(jnp.int32, (ROWS, LANES), 0)

    def extract(s, left):
        first = jnp.min(jnp.where(left != 0, place, ROWS), axis=0, keepdims=True)
        now = place == first
        code_ref[pl.ds(s, 1), :] = jnp.sum(jnp.where(now, code, 0), axis=0, keepdims=True)
        flux_ref[pl.ds(s, 1), :] = jnp.sum(jnp.where(now, flux, 0.0), axis=0, keepdims=True)
        return jnp.where(now, 0, left)

    lax.fori_loop(0, steps, extract, hit)

    def scatter(b, carry):
        rows = pl.ds(pl.multiple_of(b * 8, 8), 8)
        codes = code_ref[rows]
        parts = pieces(flux_ref[rows])
        here = lax.broadcasted_iota(jnp.int32, (B, LANES), 0)
        row_of = lax.shift_right_logical(codes, 9)
        col_of = jnp.bitwise_and(codes, 511)
        right = jnp.concatenate(
            [jnp.where(here == col_of[s : s + 1], 1.0, 0.0).astype(BF16) for s in range(8)], axis=1
        )
        total = jnp.zeros((B, B), F32)
        for part in parts:
            left = jnp.concatenate(
                [jnp.where(here == row_of[s : s + 1], part[s : s + 1], 0.0).astype(BF16) for s in range(8)],
                axis=1,
            )
            total = total + dot_nt(left, right)
        out_ref[slot] = out_ref[slot] - total
        return carry

    lax.fori_loop(0, lax.div(steps + 7, 8), scatter, 0)

    @pl.when(c == lax.rem(r, 8))
    def _():
        own = jnp.where(mine, flux, 0.0)
        parts = pieces(own)
        high = lax.shift_right_logical(low_row, 7)
        low = jnp.bitwise_and(low_row, 127)
        here8 = lax.broadcasted_iota(jnp.int32, (8, LANES), 0)
        here128 = lax.broadcasted_iota(jnp.int32, (LANES, LANES), 0)
        total = jnp.zeros((24, LANES), F32)
        for g in range(ROWS // 8):
            ones = []
            lefts = []
            for s in range(8 * g, 8 * g + 8):
                ones.append(jnp.where(here128 == low[s : s + 1], 1.0, 0.0).astype(BF16))
                at = here8 == high[s : s + 1]
                lefts.append(
                    jnp.concatenate([jnp.where(at, part[s : s + 1], 0.0) for part in parts], axis=0).astype(BF16)
                )
            total = total + dot_nt(jnp.concatenate(lefts, axis=1), jnp.concatenate(ones, axis=1))
        diagonal = total[0:8] + total[8:16] + total[16:24]
        eye = here128 == lax.broadcasted_iota(jnp.int32, (LANES, LANES), 1)
        which = jnp.where(upper, 0, 1)
        for t in range(4):
            part = pl.ds(t * LANES, LANES)
            out_ref[which, part, part] = out_ref[which, part, part] + jnp.where(eye, diagonal[t : t + 1], 0.0)


def add_weirs(base, block_mask, every_head, coef, weir_node, weir_cell):
    pad = ROWS * LANES - coef.shape[0]
    coef = jnp.pad(coef, (0, pad)).reshape(ROWS, LANES)
    node = jnp.pad(weir_node, (0, pad)).reshape(ROWS, LANES)
    cell = jnp.pad(weir_cell, (0, pad), constant_values=4096).reshape(ROWS, LANES)
    vmem = pl.BlockSpec(memory_space=pltpu.VMEM)
    return pl.pallas_call(
        weirs_kernel,
        out_shape=jax.ShapeDtypeStruct((2, B, B), F32),
        in_specs=[pl.BlockSpec(memory_space=pltpu.SMEM)] + [vmem] * 5,
        out_specs=vmem,
        scratch_shapes=[pltpu.VMEM((ROWS, LANES), jnp.int32), pltpu.VMEM((ROWS, LANES), F32)],
        compiler_params=pltpu.CompilerParams(vmem_limit_bytes=VMEM_LIMIT),
        name="add_weirs",
    )(block_mask, base, every_head, coef, node, cell)


def eliminate_kernel(
    a_ref,
    out_ref,
    side,
    panel,
    corner,
    pivot,
    ph,
    pl_,
    sh,
    sl,
    xf,
    wide_send,
    wide_recv,
    pair_send,
    pair_recv,
    side_send,
    side_recv,
    corner_sem,
    last_send,
    last_recv,
):
    r = lax.axis_index("wide")
    c = lax.axis_index("narrow")
    core = lax.rem(r, 2)
    chip = lax.div(r, 2)
    y = lax.rem(chip, 4)
    x = lax.div(chip, 4)
    z = lax.rem(c, 4)
    far = lax.div(c, 4)
    up = (x * 8 + lax.rem(y + 1, 4) * 2 + core, c)
    down = (x * 8 + lax.rem(y + 3, 4) * 2 + core, c)
    across = ((1 - x) * 8 + y * 2 + core, c)
    pair = (chip * 2 + 1 - core, c)
    ahead = (r, far * 4 + lax.rem(z + 1, 4))
    behind = (r, far * 4 + lax.rem(z + 3, 4))
    over = (r, (1 - far) * 4 + z)

    barrier = pltpu.get_barrier_semaphore()
    for peer in (up, down, across, pair, ahead, behind, over):
        pl.semaphore_signal(barrier, inc=1, device_id=peer, device_id_type=MESH)
    pl.semaphore_wait(barrier, 7)

    def loop(first, last, act):
        lax.fori_loop(first, last, lambda i, carry: (act(i), carry)[1], 0)

    def pick(values, at):
        return sum(jnp.where(at == i, v, 0) for i, v in enumerate(values) if v)

    start = lambda copy: copy.start()
    sent = lambda copy: copy.wait_send()

    depth = tuple(pick(values, chip) for values in TREE_DEPTH)
    ways = tuple(tuple(pick(values, chip) == 1 for values in tree) for tree in TREE_WAYS)

    def wide_copy(j, way, target):
        rows = pl.ds(pl.multiple_of(lax.rem(j, PARTS) * CHUNK, CHUNK), CHUNK)
        chunk = panel.at[core, lax.div(j, PARTS), rows]
        return pltpu.make_async_remote_copy(
            src_ref=chunk,
            dst_ref=chunk,
            send_sem=wide_send.at[j, way],
            recv_sem=wide_recv.at[j],
            device_id=target,
            device_id_type=MESH,
        )

    def wide_each(tree, j, act):
        for way, target in enumerate((up, down, across)):

            @pl.when(ways[tree][way])
            def _():
                act(wide_copy(j, way, target))

    def wide_slot(first, end, slot, forward=False):
        for tree in range(3):
            j = 3 * (slot - SLOTS * depth[tree]) + tree

            @pl.when((j >= first) & (j < end))
            def _():
                wide_copy(j, 0, up).wait_recv()
                wide_each(tree, j, start)
                if forward:
                    last_copy(j).start()

    def wide_relay(block, forward=False):
        first, end = block * PARTS, (block + 1) * PARTS
        loop(first // 3 - 1, (end + 2) // 3 + 4 * SLOTS, lambda slot: wide_slot(first, end, slot, forward))

    def wide_source(block, act):
        def one(j):
            for tree in range(3):

                @pl.when(lax.rem(j, 3) == tree)
                def _():
                    wide_each(tree, j, act)

        loop(block * PARTS, (block + 1) * PARTS, one)

    def pair_copy(b):
        block = panel.at[core, b]
        return pltpu.make_async_remote_copy(
            src_ref=block,
            dst_ref=block,
            send_sem=pair_send.at[b],
            recv_sem=pair_recv.at[b],
            device_id=pair,
            device_id_type=MESH,
        )

    def pair_wait(b):
        block = panel.at[1 - core, b]
        pltpu.make_async_remote_copy(
            src_ref=block,
            dst_ref=block,
            send_sem=pair_send.at[b],
            recv_sem=pair_recv.at[b],
            device_id=pair,
            device_id_type=MESH,
        ).wait_recv()

    def last_copy(j):
        rows = pl.ds(pl.multiple_of(lax.rem(j, PARTS) * CHUNK, CHUNK), CHUNK)
        chunk = panel.at[0, 4, rows]
        return pltpu.make_async_remote_copy(
            src_ref=chunk,
            dst_ref=chunk,
            send_sem=last_send.at[lax.rem(j, PARTS)],
            recv_sem=last_recv.at[lax.rem(j, PARTS)],
            device_id=pair,
            device_id_type=MESH,
        )

    def side_copy(s, j, way, target):
        chunk = side.at[s, pl.ds(pl.multiple_of(j * CHUNK, CHUNK), CHUNK)]
        return pltpu.make_async_remote_copy(
            src_ref=chunk,
            dst_ref=chunk,
            send_sem=side_send.at[s, j, way],
            recv_sem=side_recv.at[s, j],
            device_id=target,
            device_id_type=MESH,
        )

    places = tuple(far * 4 + lax.rem(z + 4 - s, 4) for s in range(2))
    side_depth = tuple(tuple(pick(values, place) for values in TREE_DEPTH) for place in places)
    side_ways = tuple(
        tuple(tuple(pick(values, place) == 1 for values in tree) for tree in TREE_WAYS) for place in places
    )

    def side_each(s, tree, j, act):
        for way, target in enumerate((ahead, behind, over)):

            @pl.when(side_ways[s][tree][way])
            def _():
                act(side_copy(s, j, way, target))

    def side_slot(slot):
        for s in range(2):
            for tree in range(3):
                j = 3 * (slot - 6 * s - SLOTS * side_depth[s][tree]) + tree

                @pl.when((j >= 0) & (j < PARTS))
                def _():
                    @pl.when(c != s)
                    def _():
                        side_copy(s, j, 0, ahead).wait_recv()

                    side_each(s, tree, j, start)

    SIDE_FIRST = 6 + 4 * SLOTS
    SIDE_END = 12 + 4 * SLOTS

    def put(index, value):
        high, low = split(value)
        ph[index] = high
        pl_[index] = low

    def times(i, j):
        return product(ph[i], pl_[i], ph[j], pl_[j])

    def invert(hook):
        here = lax.broadcasted_iota(jnp.int32, (B, B), 0) == lax.broadcasted_iota(jnp.int32, (B, B), 1)
        block = pivot[...]
        only = jnp.where(here, block, 0.0)
        one_row = 1.0 / jnp.sum(only, axis=0, keepdims=True)
        one_col = 1.0 / jnp.sum(only, axis=1, keepdims=True)
        eye = jnp.where(here, 1.0, 0.0)
        rest = eye - block * one_row
        xf[...] = one_col * (eye + rest)
        high, low = split(rest)
        sh[0, B:] = high
        sl[0, B:] = low
        high, low = split(product(sh[0, B:], sl[0, B:], sh[0, B:], sl[0, B:]))
        sh[1, B:] = high
        sl[1, B:] = low
        high, low = split(xf[...])
        sh[1, :B] = high
        sl[1, :B] = low

        def step(k):
            now = lax.rem(k, 2)
            later = 1 - now
            both = product(sh[now], sl[now], sh[now, B:], sl[now, B:])
            total = xf[...] + both[:B]
            xf[...] = total
            high, low = split(total)
            sh[later, :B] = high
            sl[later, :B] = low
            high, low = split(both[B:])
            sh[later, B:] = high
            sl[later, B:] = low
            hook(k)

        loop(1, NS_STEPS - 1, step)
        now = (NS_STEPS - 1) % 2
        return xf[...] + product(sh[now, :B], sl[now, :B], sh[now, B:], sl[now, B:])

    corner_copy = pltpu.make_async_remote_copy(
        src_ref=side.at[1],
        dst_ref=corner,
        send_sem=corner_sem.at[0],
        recv_sem=corner_sem.at[1],
        device_id=pair,
        device_id_type=MESH,
    )

    for s in range(2):

        @pl.when(c == s)
        def _():
            side[s] = a_ref[0]

    @pl.when(r < 2)
    def _():
        panel[core, 0] = a_ref[0]
        panel[core, 1] = a_ref[1]
        wide_source(0, start)
        wide_source(1, start)
        pair_copy(0).start()
        pair_copy(1).start()

    @pl.when(r == 0)
    def _():
        loop(0, SIDE_FIRST, side_slot)
        pivot[...] = side[0]

        def between(k):
            side_slot(SIDE_FIRST + 2 * k - 2)
            side_slot(SIDE_FIRST + 2 * k - 1)

            @pl.when(k == 4)
            def _():
                panel[0, 2] = side[1]
                wide_source(2, start)
                pair_copy(2).start()

        first = invert(between)
        panel[0, 3] = first
        wide_source(3, start)
        pair_copy(3).start()
        put(0, first)
        put(1, side[1])
        put(2, times(0, 1))
        pair_wait(2)
        put(3, panel[1, 2])
        corner_copy.wait_recv()
        pivot[...] = corner[...] - times(3, 2)
        panel[0, 4] = invert(lambda k: None)
        wide_source(4, start)
        loop(0, PARTS, lambda j: last_copy(j).start())
        for j in range(2):
            put(1, a_ref[j])
            out_ref[j] = times(0, 1)
        pair_wait(0)
        pair_wait(1)

    @pl.when(r == 1)
    def _():
        loop(0, SIDE_END, side_slot)
        panel[1, 2] = side[0]
        corner_copy.start()
        pair_copy(2).start()
        wide_source(2, start)

    @pl.when(r >= 2)
    def _():
        def early(slot):
            side_slot(slot)
            wide_slot(0, 2 * PARTS, slot)

        loop(0, max(SIDE_END, 11 + 4 * SLOTS), early)
        pair_copy(0).start()
        pair_copy(1).start()

    @pl.when((r >= 2) & (core == 0))
    def _():
        wide_relay(2)
        pair_copy(2).start()
        wide_relay(3)
        pair_copy(3).start()
        pair_wait(0)
        pair_wait(1)
        pair_wait(2)

    @pl.when((r >= 2) & (core == 1))
    def _():
        wide_relay(2)
        pair_copy(2).start()

    @pl.when(core == 1)
    def _():
        for b in range(4):
            pair_wait(b)

    @pl.when(r >= 1)
    def _():
        put(0, panel[0, 3])
        put(3, side[0])
        for j in range(2):
            put(1, panel[0, j])
            put(4 + j, times(0, 1))
            kept = a_ref[j] - times(3, 4 + j)
            out_ref[j] = kept

            @pl.when(r == 1)
            def _():
                put(6 + j, kept)

        @pl.when(r >= 2)
        def _():
            put(1, panel[1, 2])
            for j in range(2):
                put(6 + j, panel[1, j] - times(1, 4 + j))
            put(1, panel[0, 2])
            put(2, times(0, 1))
            put(4, side[1] - times(3, 2))

        @pl.when((r >= 2) & (core == 0))
        def _():
            wide_relay(4, forward=True)

        @pl.when(core == 1)
        def _():
            loop(0, PARTS, lambda j: last_copy(j).wait_recv())

        put(0, panel[0, 4])
        for j in range(2):
            scaled = times(0, 6 + j)
            live = c >= 2 if j == 0 else c >= 0

            @pl.when((r == 1) & live)
            def _():
                out_ref[j] = scaled

            @pl.when((r >= 2) & live)
            def _():
                put(5, scaled)
                out_ref[j] = out_ref[j] - times(4, 5)

    @pl.when(c == 0)
    def _():
        out_ref[0] = a_ref[0]

    for s in range(2):

        def one(j):
            for tree in range(3):

                @pl.when(lax.rem(j, 3) == tree)
                def _():
                    side_each(s, tree, j, sent)

        loop(0, PARTS, one)

    @pl.when(core == 0)
    def _():
        for b in range(5):
            wide_source(b, sent)
        for b in range(4):
            pair_copy(b).wait_send()
        loop(0, PARTS, lambda j: last_copy(j).wait_send())

    @pl.when(core == 1)
    def _():
        for b in range(3):
            wide_source(b, sent)
            pair_copy(b).wait_send()

    @pl.when(r == 1)
    def _():
        corner_copy.wait_send()


def eliminate(blocks):
    vmem = pl.BlockSpec(memory_space=pltpu.VMEM)
    dma = pltpu.SemaphoreType.DMA
    return pl.pallas_call(
        eliminate_kernel,
        out_shape=jax.ShapeDtypeStruct((2, B, B), F32),
        in_specs=[vmem],
        out_specs=vmem,
        scratch_shapes=[
            pltpu.VMEM((2, B, B), F32),
            pltpu.VMEM((2, 5, B, B), F32),
            pltpu.VMEM((B, B), F32),
            pltpu.VMEM((B, B), F32),
            pltpu.VMEM((8, B, B), BF16),
            pltpu.VMEM((8, B, B), BF16),
            pltpu.VMEM((2, 2 * B, B), BF16),
            pltpu.VMEM((2, 2 * B, B), BF16),
            pltpu.VMEM((B, B), F32),
            dma((5 * PARTS, 3)),
            dma((5 * PARTS,)),
            dma((4,)),
            dma((4,)),
            dma((2, PARTS, 3)),
            dma((2, PARTS)),
            dma((2,)),
            dma((PARTS,)),
            dma((PARTS,)),
        ],
        compiler_params=pltpu.CompilerParams(
            collective_id=1, has_side_effects=True, vmem_limit_bytes=VMEM_LIMIT
        ),
        name="eliminate",
    )(blocks)


def per_device(base, block_mask, heads, coef, weir_node, weir_cell):
    blocks = base.reshape(2, B, B)
    every_head = gather_heads(heads)
    blocks = add_weirs(blocks, block_mask, every_head, coef, weir_node, weir_cell)
    return eliminate(blocks).reshape(base.shape)


def solution(mesh):
    placed = (P(None, "wide", None, "narrow", None, None), P(), P("narrow"), P(), P(), P())
    return jax.shard_map(
        per_device,
        mesh=mesh,
        in_specs=placed,
        out_specs=P(None, "wide", None, "narrow", None, None),
        check_vma=False,
    )
```

```python
import functools

import jax
import jax.numpy as jnp
from jax import lax
from jax.experimental import pallas as pl
from jax.experimental.pallas import tpu as pltpu
from jax.sharding import PartitionSpec as P

NS_STEPS = 6
B = 512
ROWS = 72
LANES = 128
MESH = pl.DeviceIdType.MESH
F32 = jnp.float32
BF16 = jnp.bfloat16
VMEM_LIMIT = 56 * 2**20
SLOTS = 2
CHUNK = 64
PARTS = B // CHUNK
TREE_DEPTH = ((0, 1, 2, 3, 3, 2, 3, 4), (0, 3, 2, 1, 3, 4, 3, 2), (0, 3, 4, 3, 1, 2, 3, 2))
TREE_WAYS = (
    ((1, 1, 1, 0, 0, 0, 1, 0), (0, 0, 0, 0, 0, 1, 0, 0), (0, 1, 1, 0, 0, 0, 0, 0)),
    ((0, 0, 0, 0, 0, 0, 0, 1), (1, 0, 1, 1, 0, 0, 1, 1), (0, 0, 0, 1, 0, 0, 0, 0)),
    ((0, 0, 0, 0, 1, 1, 0, 0), (0, 0, 0, 0, 1, 0, 0, 0), (1, 0, 0, 0, 0, 1, 1, 1)),
)


def split(x):
    high = x.astype(BF16)
    return high, (x - high.astype(F32)).astype(BF16)


def dot(a, b):
    return jnp.dot(a, b, preferred_element_type=F32)


def dot_nt(a, b):
    return lax.dot_general(a, b, (((1,), (1,)), ((), ())), preferred_element_type=F32)


def product(ah, al, bh, bl):
    return dot(ah, bh) + dot(ah, bl) + dot(al, bh)


def gather_heads_kernel(mine_ref, every_ref, send_sem, recv_sem):
    r = lax.axis_index("wide")
    c = lax.axis_index("narrow")
    count = 8
    barrier = pltpu.get_barrier_semaphore()
    for hop in range(1, count):
        pl.semaphore_signal(barrier, inc=1, device_id=(r, lax.rem(c + hop, count)), device_id_type=MESH)
    pl.semaphore_wait(barrier, count - 1)
    place = pl.ds(pl.multiple_of(c * 8, 8), 8)
    copies = []
    for hop in range(1, count):
        copy = pltpu.make_async_remote_copy(
            src_ref=mine_ref,
            dst_ref=every_ref.at[place],
            send_sem=send_sem.at[hop],
            recv_sem=recv_sem.at[hop],
            device_id=(r, lax.rem(c + hop, count)),
            device_id_type=MESH,
        )
        copy.start()
        copies.append(copy)
    every_ref[place] = mine_ref[...]
    for copy in copies:
        copy.wait()


def gather_heads(heads):
    return pl.pallas_call(
        gather_heads_kernel,
        out_shape=jax.ShapeDtypeStruct((64, LANES), F32),
        in_specs=[pl.BlockSpec(memory_space=pltpu.VMEM)],
        out_specs=pl.BlockSpec(memory_space=pltpu.VMEM),
        scratch_shapes=[pltpu.SemaphoreType.DMA((8,)), pltpu.SemaphoreType.DMA((8,))],
        compiler_params=pltpu.CompilerParams(collective_id=0, has_side_effects=True),
        name="gather_heads",
    )(heads.reshape(8, LANES))


def lookup(table_ref, first, index):
    high = lax.shift_right_logical(index, 7) - first
    low = jnp.bitwise_and(index, 127)
    found = jnp.zeros(index.shape, F32)
    for t in range(32):
        row = jnp.broadcast_to(table_ref[pl.ds(first + t, 1), :], index.shape)
        picked = jnp.take_along_axis(row, low, axis=1, mode="promise_in_bounds")
        found = jnp.where(high == t, picked, found)
    return found


def pieces(x):
    high = x.astype(BF16).astype(F32)
    rest = x - high
    middle = rest.astype(BF16).astype(F32)
    return high, middle, rest - middle


def weirs_kernel(mask_ref, base_ref, heads_ref, coef_ref, node_ref, cell_ref, out_ref, code_ref, flux_ref):
    r = lax.axis_index("wide")
    c = lax.axis_index("narrow")
    upper = r < 8
    for j in range(2):
        col = c + 8 * j
        keep = jnp.where((mask_ref[r, col] != 0) | (r == col), 1.0, 0.0).astype(F32)
        out_ref[j] = base_ref[j] * keep
    node = node_ref[...]
    cell = cell_ref[...]
    drop = lookup(heads_ref, 0, node) - lookup(heads_ref, 32, cell)
    flux = 1.5 * coef_ref[...] * jnp.sqrt(drop * drop + 0.01)
    row = jnp.where(upper, node, cell)
    col = jnp.where(upper, cell, node)
    mine = lax.shift_right_logical(row, 9) == r
    low_row = jnp.bitwise_and(row, 511)

    target = jnp.where(upper, c + 8, c)
    slot = jnp.where(upper, 1, 0)
    hit = jnp.where(mine & (lax.shift_right_logical(col, 9) == target), 1, 0)
    code = low_row * 512 + jnp.bitwise_and(col, 511)
    steps = jnp.max(jnp.sum(hit.astype(F32), axis=0, keepdims=True)).astype(jnp.int32)
    code_ref[...] = jnp.zeros(code_ref.shape, jnp.int32)
    flux_ref[...] = jnp.zeros(flux_ref.shape, F32)
    place = lax.broadcasted_iota(jnp.int32, (ROWS, LANES), 0)

    def extract(s, left):
        first = jnp.min(jnp.where(left != 0, place, ROWS), axis=0, keepdims=True)
        now = place == first
        code_ref[pl.ds(s, 1), :] = jnp.sum(jnp.where(now, code, 0), axis=0, keepdims=True)
        flux_ref[pl.ds(s, 1), :] = jnp.sum(jnp.where(now, flux, 0.0), axis=0, keepdims=True)
        return jnp.where(now, 0, left)

    lax.fori_loop(0, steps, extract, hit)

    def scatter(b, carry):
        rows = pl.ds(pl.multiple_of(b * 8, 8), 8)
        codes = code_ref[rows]
        parts = pieces(flux_ref[rows])
        here = lax.broadcasted_iota(jnp.int32, (B, LANES), 0)
        row_of = lax.shift_right_logical(codes, 9)
        col_of = jnp.bitwise_and(codes, 511)
        right = jnp.concatenate(
            [jnp.where(here == col_of[s : s + 1], 1.0, 0.0).astype(BF16) for s in range(8)], axis=1
        )
        total = jnp.zeros((B, B), F32)
        for part in parts:
            left = jnp.concatenate(
                [jnp.where(here == row_of[s : s + 1], part[s : s + 1], 0.0).astype(BF16) for s in range(8)],
                axis=1,
            )
            total = total + dot_nt(left, right)
        out_ref[slot] = out_ref[slot] - total
        return carry

    lax.fori_loop(0, lax.div(steps + 7, 8), scatter, 0)

    @pl.when(c == lax.rem(r, 8))
    def _():
        own = jnp.where(mine, flux, 0.0)
        parts = pieces(own)
        high = lax.shift_right_logical(low_row, 7)
        low = jnp.bitwise_and(low_row, 127)
        here8 = lax.broadcasted_iota(jnp.int32, (8, LANES), 0)
        here128 = lax.broadcasted_iota(jnp.int32, (LANES, LANES), 0)
        total = jnp.zeros((24, LANES), F32)
        for g in range(ROWS // 8):
            ones = []
            lefts = []
            for s in range(8 * g, 8 * g + 8):
                ones.append(jnp.where(here128 == low[s : s + 1], 1.0, 0.0).astype(BF16))
                at = here8 == high[s : s + 1]
                lefts.append(
                    jnp.concatenate([jnp.where(at, part[s : s + 1], 0.0) for part in parts], axis=0).astype(BF16)
                )
            total = total + dot_nt(jnp.concatenate(lefts, axis=1), jnp.concatenate(ones, axis=1))
        diagonal = total[0:8] + total[8:16] + total[16:24]
        eye = here128 == lax.broadcasted_iota(jnp.int32, (LANES, LANES), 1)
        which = jnp.where(upper, 0, 1)
        for t in range(4):
            part = pl.ds(t * LANES, LANES)
            out_ref[which, part, part] = out_ref[which, part, part] + jnp.where(eye, diagonal[t : t + 1], 0.0)


def add_weirs(base, block_mask, every_head, coef, weir_node, weir_cell):
    pad = ROWS * LANES - coef.shape[0]
    coef = jnp.pad(coef, (0, pad)).reshape(ROWS, LANES)
    node = jnp.pad(weir_node, (0, pad)).reshape(ROWS, LANES)
    cell = jnp.pad(weir_cell, (0, pad), constant_values=4096).reshape(ROWS, LANES)
    vmem = pl.BlockSpec(memory_space=pltpu.VMEM)
    return pl.pallas_call(
        weirs_kernel,
        out_shape=jax.ShapeDtypeStruct((2, B, B), F32),
        in_specs=[pl.BlockSpec(memory_space=pltpu.SMEM)] + [vmem] * 5,
        out_specs=vmem,
        scratch_shapes=[pltpu.VMEM((ROWS, LANES), jnp.int32), pltpu.VMEM((ROWS, LANES), F32)],
        compiler_params=pltpu.CompilerParams(vmem_limit_bytes=VMEM_LIMIT),
        name="add_weirs",
    )(block_mask, base, every_head, coef, node, cell)


def eliminate_kernel(
    a_ref,
    out_ref,
    side,
    panel,
    direct,
    pivot,
    ph,
    pl_,
    sh,
    sl,
    xf,
    wide_send,
    wide_recv,
    pair_send,
    pair_recv,
    side_send,
    side_recv,
    direct_send,
    direct_recv,
    inverse_send,
    inverse_recv,
    last_send,
    last_recv,
):
    r = lax.axis_index("wide")
    c = lax.axis_index("narrow")
    core = lax.rem(r, 2)
    chip = lax.div(r, 2)
    y = lax.rem(chip, 4)
    x = lax.div(chip, 4)
    z = lax.rem(c, 4)
    far = lax.div(c, 4)
    up = (x * 8 + lax.rem(y + 1, 4) * 2 + core, c)
    down = (x * 8 + lax.rem(y + 3, 4) * 2 + core, c)
    across = ((1 - x) * 8 + y * 2 + core, c)
    pair = (chip * 2 + 1 - core, c)
    ahead = (r, far * 4 + lax.rem(z + 1, 4))
    behind = (r, far * 4 + lax.rem(z + 3, 4))
    over = (r, (1 - far) * 4 + z)

    barrier = pltpu.get_barrier_semaphore()
    for peer in (up, down, across, pair, ahead, behind, over):
        pl.semaphore_signal(barrier, inc=1, device_id=peer, device_id_type=MESH)
    pl.semaphore_wait(barrier, 7)

    def loop(first, last, act):
        lax.fori_loop(first, last, lambda i, carry: (act(i), carry)[1], 0)

    def pick(values, at):
        return sum(jnp.where(at == i, v, 0) for i, v in enumerate(values) if v)

    start = lambda copy: copy.start()
    sent = lambda copy: copy.wait_send()

    depth = tuple(pick(values, chip) for values in TREE_DEPTH)
    ways = tuple(tuple(pick(values, chip) == 1 for values in tree) for tree in TREE_WAYS)

    def wide_copy(j, way, target):
        rows = pl.ds(pl.multiple_of(lax.rem(j, PARTS) * CHUNK, CHUNK), CHUNK)
        chunk = panel.at[core, lax.div(j, PARTS), rows]
        return pltpu.make_async_remote_copy(
            src_ref=chunk,
            dst_ref=chunk,
            send_sem=wide_send.at[j, way],
            recv_sem=wide_recv.at[j],
            device_id=target,
            device_id_type=MESH,
        )

    def wide_each(tree, j, act):
        for way, target in enumerate((up, down, across)):

            @pl.when(ways[tree][way])
            def _():
                act(wide_copy(j, way, target))

    def wide_slot(first, end, slot, forward=False):
        for tree in range(3):
            j = 3 * (slot - SLOTS * depth[tree]) + tree

            @pl.when((j >= first) & (j < end))
            def _():
                wide_copy(j, 0, up).wait_recv()
                wide_each(tree, j, start)
                if forward:
                    last_copy(j).start()

    def wide_relay(first_block, end_block, forward=False):
        first, end = first_block * PARTS, end_block * PARTS
        loop(first // 3 - 1, (end + 2) // 3 + 4 * SLOTS, lambda slot: wide_slot(first, end, slot, forward))

    def wide_source(block, act):
        def one(j):
            for tree in range(3):

                @pl.when(lax.rem(j, 3) == tree)
                def _():
                    wide_each(tree, j, act)

        loop(block * PARTS, (block + 1) * PARTS, one)

    def pair_copy(b):
        block = panel.at[core, b]
        return pltpu.make_async_remote_copy(
            src_ref=block,
            dst_ref=block,
            send_sem=pair_send.at[b],
            recv_sem=pair_recv.at[b],
            device_id=pair,
            device_id_type=MESH,
        )

    def pair_wait(b):
        block = panel.at[1 - core, b]
        pltpu.make_async_remote_copy(
            src_ref=block,
            dst_ref=block,
            send_sem=pair_send.at[b],
            recv_sem=pair_recv.at[b],
            device_id=pair,
            device_id_type=MESH,
        ).wait_recv()

    def last_copy(j):
        rows = pl.ds(pl.multiple_of(lax.rem(j, PARTS) * CHUNK, CHUNK), CHUNK)
        chunk = panel.at[0, 3, rows]
        return pltpu.make_async_remote_copy(
            src_ref=chunk,
            dst_ref=chunk,
            send_sem=last_send.at[lax.rem(j, PARTS)],
            recv_sem=last_recv.at[lax.rem(j, PARTS)],
            device_id=pair,
            device_id_type=MESH,
        )

    def side_copy(s, j, way, target):
        chunk = side.at[s, pl.ds(pl.multiple_of(j * CHUNK, CHUNK), CHUNK)]
        return pltpu.make_async_remote_copy(
            src_ref=chunk,
            dst_ref=chunk,
            send_sem=side_send.at[s, j, way],
            recv_sem=side_recv.at[s, j],
            device_id=target,
            device_id_type=MESH,
        )

    places = tuple(far * 4 + lax.rem(z + 4 - s, 4) for s in range(2))
    side_depth = [[pick(values, place) for values in TREE_DEPTH] for place in places]
    side_ways = [
        [[pick(values, place) for values in tree] for tree in TREE_WAYS] for place in places
    ]
    side_depth[1][1] = jnp.where(r == 0, side_depth[1][2], side_depth[1][1])
    side_ways[1][1] = [jnp.where(r == 0, v2, v1) for v1, v2 in zip(side_ways[1][1], side_ways[1][2])]

    def side_each(s, tree, j, act):
        for way, target in enumerate((ahead, behind, over)):

            @pl.when(side_ways[s][tree][way] == 1)
            def _():
                act(side_copy(s, j, way, target))

    def side_slot(slot, panels):
        for s in panels:
            for tree in range(3):
                j = 3 * (slot - 3 * s - SLOTS * side_depth[s][tree]) + tree

                @pl.when((j >= 0) & (j < PARTS))
                def _():
                    @pl.when(c != s)
                    def _():
                        side_copy(s, j, 0, ahead).wait_recv()

                    side_each(s, tree, j, start)

    SIDE_END = 6 + 4 * SLOTS

    def inverse_copy(b, j, way, target):
        chunk = panel.at[0, b, pl.ds(pl.multiple_of(j * CHUNK, CHUNK), CHUNK)]
        return pltpu.make_async_remote_copy(
            src_ref=chunk,
            dst_ref=chunk,
            send_sem=inverse_send.at[b - 2, j, way],
            recv_sem=inverse_recv.at[b - 2, j],
            device_id=target,
            device_id_type=MESH,
        )

    def inverse_each(b, tree, j, act):
        for way, target in enumerate((ahead, behind, over)):

            @pl.when(side_ways[0][tree][way] == 1)
            def _():
                act(inverse_copy(b, j, way, target))

    def inverse_slot(b, slot):
        for tree in range(3):
            j = 3 * (slot - SLOTS * side_depth[0][tree]) + tree

            @pl.when((j >= 0) & (j < PARTS))
            def _():
                @pl.when(c != 0)
                def _():
                    inverse_copy(b, j, 0, ahead).wait_recv()

                inverse_each(b, tree, j, start)
                for kind in range(3):

                    @pl.when(lax.rem(b * PARTS + j, 3) == kind)
                    def _():
                        wide_each(kind, b * PARTS + j, start)

    INVERSE_LATER = 4
    INVERSE_END = (PARTS + 2) // 3 + 4 * SLOTS

    def inverse_pass(b):
        loop(0, INVERSE_END, lambda slot: inverse_slot(b, slot))

    def put(index, value):
        high, low = split(value)
        ph[index] = high
        pl_[index] = low

    def times(i, j):
        return product(ph[i], pl_[i], ph[j], pl_[j])

    def invert():
        here = lax.broadcasted_iota(jnp.int32, (B, B), 0) == lax.broadcasted_iota(jnp.int32, (B, B), 1)
        block = pivot[...]
        only = jnp.where(here, block, 0.0)
        one_row = 1.0 / jnp.sum(only, axis=0, keepdims=True)
        one_col = 1.0 / jnp.sum(only, axis=1, keepdims=True)
        eye = jnp.where(here, 1.0, 0.0)
        rest = eye - block * one_row
        xf[...] = one_col * (eye + rest)
        high, low = split(rest)
        sh[0, B:] = high
        sl[0, B:] = low
        high, low = split(product(sh[0, B:], sl[0, B:], sh[0, B:], sl[0, B:]))
        sh[1, B:] = high
        sl[1, B:] = low
        high, low = split(xf[...])
        sh[1, :B] = high
        sl[1, :B] = low

        def step(k):
            now = lax.rem(k, 2)
            later = 1 - now
            both = product(sh[now], sl[now], sh[now, B:], sl[now, B:])
            total = xf[...] + both[:B]
            xf[...] = total
            high, low = split(total)
            sh[later, :B] = high
            sl[later, :B] = low
            high, low = split(both[B:])
            sh[later, B:] = high
            sl[later, B:] = low

        loop(1, NS_STEPS - 1, step)
        now = (NS_STEPS - 1) % 2
        return xf[...] + product(sh[now, :B], sl[now, :B], sh[now, B:], sl[now, B:])

    def direct_copy(src, dst, at, target):
        return pltpu.make_async_remote_copy(
            src_ref=src,
            dst_ref=dst,
            send_sem=direct_send.at[at],
            recv_sem=direct_recv.at[at],
            device_id=target,
            device_id_type=MESH,
        )

    first_copy = direct_copy(side.at[1], direct.at[0], 0, behind)
    second_copy = direct_copy(direct.at[1], direct.at[1], 1, behind)
    corner_copy = direct_copy(side.at[1], direct.at[1], 2, pair)
    cross_copy = direct_copy(side.at[1], panel.at[1, 3], 3, pair)
    cross_first = direct_copy(direct.at[0], panel.at[1, 3], 3, pair)

    for s in range(2):

        @pl.when(c == s)
        def _():
            side[s] = a_ref[0]

    @pl.when(r < 2)
    def _():
        panel[core, 0] = a_ref[0]
        panel[core, 1] = a_ref[1]
        wide_source(0, start)
        wide_source(1, start)
        pair_copy(0).start()
        pair_copy(1).start()

    @pl.when((r == 1) & (c == 1))
    def _():
        corner_copy.start()

    @pl.when((r == 0) & (c == 1))
    def _():
        first_copy.start()
        corner_copy.wait_recv()
        second_copy.start()

    @pl.when((r == 0) & (c == 0))
    def _():
        pivot[...] = side[0]
        first = invert()
        panel[0, 2] = first
        inverse_pass(2)
        pair_copy(2).start()
        put(0, first)
        first_copy.wait_recv()
        cross_first.start()
        put(1, direct[0])
        put(2, times(0, 1))
        pair_wait(2)
        put(3, panel[1, 2])
        second_copy.wait_recv()
        pivot[...] = direct[1] - times(3, 2)
        panel[0, 3] = invert()
        inverse_pass(3)
        loop(0, PARTS, lambda j: last_copy(j).start())
        loop(0, SIDE_END, lambda slot: side_slot(slot, (1,)))

    @pl.when((r == 0) & (c != 0))
    def _():
        def both(slot):
            side_slot(slot, (1,))

            @pl.when(slot == SIDE_END - 1)
            def _():
                cross_copy.start()

            inverse_slot(2, slot - INVERSE_LATER)

        loop(0, INVERSE_END + INVERSE_LATER, both)
        pair_copy(2).start()
        inverse_pass(3)
        loop(0, PARTS, lambda j: last_copy(j).start())
        pair_wait(2)

    @pl.when(r == 0)
    def _():
        put(0, panel[0, 2])
        for j in range(2):
            put(1, a_ref[j])
            out_ref[j] = times(0, 1)
        pair_wait(0)
        pair_wait(1)
        pair_wait(3)

    @pl.when(r == 1)
    def _():
        @pl.when(c == 0)
        def _():
            panel[1, 2] = side[0]
            pair_copy(2).start()

        loop(0, SIDE_END, lambda slot: side_slot(slot, (0,)))

        @pl.when(c != 0)
        def _():
            panel[1, 2] = side[0]
            pair_copy(2).start()

        wide_source(2, start)
        cross_copy.wait_recv()
        wide_source(3, start)
        pair_copy(3).start()

    @pl.when(r >= 2)
    def _():
        def early(slot):
            side_slot(slot, (0, 1))
            wide_slot(0, 2 * PARTS, slot)

        loop(0, SIDE_END, early)
        pair_copy(0).start()
        pair_copy(1).start()

    @pl.when((r >= 2) & (core == 0))
    def _():
        wide_relay(2, 3)
        pair_copy(2).start()
        for b in range(3):
            pair_wait(b)

    @pl.when((r >= 2) & (core == 1))
    def _():
        wide_relay(2, 4)
        pair_copy(2).start()
        pair_copy(3).start()

    @pl.when(core == 1)
    def _():
        for b in range(3):
            pair_wait(b)

    @pl.when(r >= 1)
    def _():
        put(0, panel[0, 2])
        put(3, side[0])
        for j in range(2):
            put(1, panel[0, j])
            put(4 + j, times(0, 1))
            kept = a_ref[j] - times(3, 4 + j)
            out_ref[j] = kept

            @pl.when(r == 1)
            def _():
                put(6 + j, kept)

        @pl.when(r >= 2)
        def _():
            put(1, panel[1, 2])
            for j in range(2):
                put(6 + j, panel[1, j] - times(1, 4 + j))

            @pl.when(core == 0)
            def _():
                pair_wait(3)

            put(1, panel[1, 3])
            put(2, times(0, 1))
            put(4, side[1] - times(3, 2))

        @pl.when((r >= 2) & (core == 0))
        def _():
            wide_relay(3, 4, forward=True)

        @pl.when(core == 1)
        def _():
            loop(0, PARTS, lambda j: last_copy(j).wait_recv())

        put(0, panel[0, 3])
        for j in range(2):
            scaled = times(0, 6 + j)
            live = c >= 2 if j == 0 else c >= 0

            @pl.when((r == 1) & live)
            def _():
                out_ref[j] = scaled

            @pl.when((r >= 2) & live)
            def _():
                put(5, scaled)
                out_ref[j] = out_ref[j] - times(4, 5)

    @pl.when(c == 0)
    def _():
        out_ref[0] = a_ref[0]

    def side_sent(s):
        def one(j):
            for tree in range(3):

                @pl.when(lax.rem(j, 3) == tree)
                def _():
                    side_each(s, tree, j, sent)

        loop(0, PARTS, one)

    @pl.when(r >= 1)
    def _():
        side_sent(0)

    @pl.when(r != 1)
    def _():
        side_sent(1)

    @pl.when(r == 0)
    def _():
        def one(j):
            for tree in range(3):

                @pl.when(lax.rem(j, 3) == tree)
                def _():
                    inverse_each(2, tree, j, sent)
                    inverse_each(3, tree, j, sent)

        loop(0, PARTS, one)
        cross_copy.wait_send()

        @pl.when(c == 1)
        def _():
            first_copy.wait_send()
            second_copy.wait_send()

    for b in range(4):
        wide_source(b, sent)
    for b in range(3):
        pair_copy(b).wait_send()

    @pl.when(core == 0)
    def _():
        loop(0, PARTS, lambda j: last_copy(j).wait_send())

    @pl.when(core == 1)
    def _():
        pair_copy(3).wait_send()

    @pl.when((r == 1) & (c == 1))
    def _():
        corner_copy.wait_send()


def eliminate(blocks):
    vmem = pl.BlockSpec(memory_space=pltpu.VMEM)
    dma = pltpu.SemaphoreType.DMA
    return pl.pallas_call(
        eliminate_kernel,
        out_shape=jax.ShapeDtypeStruct((2, B, B), F32),
        in_specs=[vmem],
        out_specs=vmem,
        scratch_shapes=[
            pltpu.VMEM((2, B, B), F32),
            pltpu.VMEM((2, 4, B, B), F32),
            pltpu.VMEM((2, B, B), F32),
            pltpu.VMEM((B, B), F32),
            pltpu.VMEM((8, B, B), BF16),
            pltpu.VMEM((8, B, B), BF16),
            pltpu.VMEM((2, 2 * B, B), BF16),
            pltpu.VMEM((2, 2 * B, B), BF16),
            pltpu.VMEM((B, B), F32),
            dma((4 * PARTS, 3)),
            dma((4 * PARTS,)),
            dma((4,)),
            dma((4,)),
            dma((2, PARTS, 3)),
            dma((2, PARTS)),
            dma((4,)),
            dma((4,)),
            dma((2, PARTS, 3)),
            dma((2, PARTS)),
            dma((PARTS,)),
            dma((PARTS,)),
        ],
        compiler_params=pltpu.CompilerParams(
            collective_id=1, has_side_effects=True, vmem_limit_bytes=VMEM_LIMIT
        ),
        name="eliminate",
    )(blocks)


def per_device(base, block_mask, heads, coef, weir_node, weir_cell):
    blocks = base.reshape(2, B, B)
    every_head = gather_heads(heads)
    blocks = add_weirs(blocks, block_mask, every_head, coef, weir_node, weir_cell)
    return eliminate(blocks).reshape(base.shape)


def solution(mesh):
    placed = (P(None, "wide", None, "narrow", None, None), P(), P("narrow"), P(), P(), P())
    return jax.shard_map(
        per_device,
        mesh=mesh,
        in_specs=placed,
        out_specs=P(None, "wide", None, "narrow", None, None),
        check_vma=False,
    )
```

```python
import functools

import jax
import jax.numpy as jnp
from jax import lax
from jax.experimental import pallas as pl
from jax.experimental.pallas import tpu as pltpu
from jax.sharding import PartitionSpec as P

NS_STEPS = 6
B = 512
ROWS = 72
LANES = 128
MESH = pl.DeviceIdType.MESH
F32 = jnp.float32
BF16 = jnp.bfloat16
VMEM_LIMIT = 56 * 2**20
SLOTS = 2
CHUNK = 64
PARTS = B // CHUNK
TREE_DEPTH = ((0, 1, 2, 3, 3, 2, 3, 4), (0, 3, 2, 1, 3, 4, 3, 2), (0, 3, 4, 3, 1, 2, 3, 2))
TREE_WAYS = (
    ((1, 1, 1, 0, 0, 0, 1, 0), (0, 0, 0, 0, 0, 1, 0, 0), (0, 1, 1, 0, 0, 0, 0, 0)),
    ((0, 0, 0, 0, 0, 0, 0, 1), (1, 0, 1, 1, 0, 0, 1, 1), (0, 0, 0, 1, 0, 0, 0, 0)),
    ((0, 0, 0, 0, 1, 1, 0, 0), (0, 0, 0, 0, 1, 0, 0, 0), (1, 0, 0, 0, 0, 1, 1, 1)),
)


def split(x):
    high = x.astype(BF16)
    return high, (x - high.astype(F32)).astype(BF16)


def dot(a, b):
    return jnp.dot(a, b, preferred_element_type=F32)


def dot_nt(a, b):
    return lax.dot_general(a, b, (((1,), (1,)), ((), ())), preferred_element_type=F32)


def product(ah, al, bh, bl):
    return dot(ah, bh) + dot(ah, bl) + dot(al, bh)


def gather_heads_kernel(mine_ref, every_ref, send_sem, recv_sem):
    r = lax.axis_index("wide")
    c = lax.axis_index("narrow")
    count = 8
    barrier = pltpu.get_barrier_semaphore()
    for hop in range(1, count):
        pl.semaphore_signal(barrier, inc=1, device_id=(r, lax.rem(c + hop, count)), device_id_type=MESH)
    pl.semaphore_wait(barrier, count - 1)
    place = pl.ds(pl.multiple_of(c * 8, 8), 8)
    copies = []
    for hop in range(1, count):
        copy = pltpu.make_async_remote_copy(
            src_ref=mine_ref,
            dst_ref=every_ref.at[place],
            send_sem=send_sem.at[hop],
            recv_sem=recv_sem.at[hop],
            device_id=(r, lax.rem(c + hop, count)),
            device_id_type=MESH,
        )
        copy.start()
        copies.append(copy)
    every_ref[place] = mine_ref[...]
    for copy in copies:
        copy.wait()


def gather_heads(heads):
    return pl.pallas_call(
        gather_heads_kernel,
        out_shape=jax.ShapeDtypeStruct((64, LANES), F32),
        in_specs=[pl.BlockSpec(memory_space=pltpu.VMEM)],
        out_specs=pl.BlockSpec(memory_space=pltpu.VMEM),
        scratch_shapes=[pltpu.SemaphoreType.DMA((8,)), pltpu.SemaphoreType.DMA((8,))],
        compiler_params=pltpu.CompilerParams(collective_id=0, has_side_effects=True),
        name="gather_heads",
    )(heads.reshape(8, LANES))


def lookup(table_ref, first, index):
    high = lax.shift_right_logical(index, 7) - first
    low = jnp.bitwise_and(index, 127)
    found = jnp.zeros(index.shape, F32)
    for t in range(32):
        row = jnp.broadcast_to(table_ref[pl.ds(first + t, 1), :], index.shape)
        picked = jnp.take_along_axis(row, low, axis=1, mode="promise_in_bounds")
        found = jnp.where(high == t, picked, found)
    return found


def pieces(x):
    high = x.astype(BF16).astype(F32)
    rest = x - high
    middle = rest.astype(BF16).astype(F32)
    return high, middle, rest - middle


def weirs_kernel(mask_ref, base_ref, heads_ref, coef_ref, node_ref, cell_ref, out_ref, code_ref, flux_ref):
    r = lax.axis_index("wide")
    c = lax.axis_index("narrow")
    upper = r < 8
    for j in range(2):
        col = c + 8 * j
        keep = jnp.where((mask_ref[r, col] != 0) | (r == col), 1.0, 0.0).astype(F32)
        out_ref[j] = base_ref[j] * keep
    node = node_ref[...]
    cell = cell_ref[...]
    drop = lookup(heads_ref, 0, node) - lookup(heads_ref, 32, cell)
    flux = 1.5 * coef_ref[...] * jnp.sqrt(drop * drop + 0.01)
    row = jnp.where(upper, node, cell)
    col = jnp.where(upper, cell, node)
    mine = lax.shift_right_logical(row, 9) == r
    low_row = jnp.bitwise_and(row, 511)

    target = jnp.where(upper, c + 8, c)
    slot = jnp.where(upper, 1, 0)
    hit = jnp.where(mine & (lax.shift_right_logical(col, 9) == target), 1, 0)
    code = low_row * 512 + jnp.bitwise_and(col, 511)
    steps = jnp.max(jnp.sum(hit.astype(F32), axis=0, keepdims=True)).astype(jnp.int32)
    code_ref[...] = jnp.zeros(code_ref.shape, jnp.int32)
    flux_ref[...] = jnp.zeros(flux_ref.shape, F32)
    place = lax.broadcasted_iota(jnp.int32, (ROWS, LANES), 0)

    def extract(s, left):
        first = jnp.min(jnp.where(left != 0, place, ROWS), axis=0, keepdims=True)
        now = place == first
        code_ref[pl.ds(s, 1), :] = jnp.sum(jnp.where(now, code, 0), axis=0, keepdims=True)
        flux_ref[pl.ds(s, 1), :] = jnp.sum(jnp.where(now, flux, 0.0), axis=0, keepdims=True)
        return jnp.where(now, 0, left)

    lax.fori_loop(0, steps, extract, hit)

    def scatter(b, carry):
        rows = pl.ds(pl.multiple_of(b * 8, 8), 8)
        codes = code_ref[rows]
        parts = pieces(flux_ref[rows])
        here = lax.broadcasted_iota(jnp.int32, (B, LANES), 0)
        row_of = lax.shift_right_logical(codes, 9)
        col_of = jnp.bitwise_and(codes, 511)
        right = jnp.concatenate(
            [jnp.where(here == col_of[s : s + 1], 1.0, 0.0).astype(BF16) for s in range(8)], axis=1
        )
        total = jnp.zeros((B, B), F32)
        for part in parts:
            left = jnp.concatenate(
                [jnp.where(here == row_of[s : s + 1], part[s : s + 1], 0.0).astype(BF16) for s in range(8)],
                axis=1,
            )
            total = total + dot_nt(left, right)
        out_ref[slot] = out_ref[slot] - total
        return carry

    lax.fori_loop(0, lax.div(steps + 7, 8), scatter, 0)

    @pl.when(c == lax.rem(r, 8))
    def _():
        own = jnp.where(mine, flux, 0.0)
        parts = pieces(own)
        high = lax.shift_right_logical(low_row, 7)
        low = jnp.bitwise_and(low_row, 127)
        here8 = lax.broadcasted_iota(jnp.int32, (8, LANES), 0)
        here128 = lax.broadcasted_iota(jnp.int32, (LANES, LANES), 0)
        total = jnp.zeros((24, LANES), F32)
        for g in range(ROWS // 8):
            ones = []
            lefts = []
            for s in range(8 * g, 8 * g + 8):
                ones.append(jnp.where(here128 == low[s : s + 1], 1.0, 0.0).astype(BF16))
                at = here8 == high[s : s + 1]
                lefts.append(
                    jnp.concatenate([jnp.where(at, part[s : s + 1], 0.0) for part in parts], axis=0).astype(BF16)
                )
            total = total + dot_nt(jnp.concatenate(lefts, axis=1), jnp.concatenate(ones, axis=1))
        diagonal = total[0:8] + total[8:16] + total[16:24]
        eye = here128 == lax.broadcasted_iota(jnp.int32, (LANES, LANES), 1)
        which = jnp.where(upper, 0, 1)
        for t in range(4):
            part = pl.ds(t * LANES, LANES)
            out_ref[which, part, part] = out_ref[which, part, part] + jnp.where(eye, diagonal[t : t + 1], 0.0)


def add_weirs(base, block_mask, every_head, coef, weir_node, weir_cell):
    pad = ROWS * LANES - coef.shape[0]
    coef = jnp.pad(coef, (0, pad)).reshape(ROWS, LANES)
    node = jnp.pad(weir_node, (0, pad)).reshape(ROWS, LANES)
    cell = jnp.pad(weir_cell, (0, pad), constant_values=4096).reshape(ROWS, LANES)
    vmem = pl.BlockSpec(memory_space=pltpu.VMEM)
    return pl.pallas_call(
        weirs_kernel,
        out_shape=jax.ShapeDtypeStruct((2, B, B), F32),
        in_specs=[pl.BlockSpec(memory_space=pltpu.SMEM)] + [vmem] * 5,
        out_specs=vmem,
        scratch_shapes=[pltpu.VMEM((ROWS, LANES), jnp.int32), pltpu.VMEM((ROWS, LANES), F32)],
        compiler_params=pltpu.CompilerParams(vmem_limit_bytes=VMEM_LIMIT),
        name="add_weirs",
    )(block_mask, base, every_head, coef, node, cell)


def eliminate_kernel(
    a_ref,
    out_ref,
    side,
    panel,
    direct,
    pivot,
    ph,
    pl_,
    sh,
    sl,
    xf,
    wide_send,
    wide_recv,
    pair_send,
    pair_recv,
    side_send,
    side_recv,
    direct_send,
    direct_recv,
    through_send,
    through_recv,
    last_send,
    last_recv,
):
    r = lax.axis_index("wide")
    c = lax.axis_index("narrow")
    core = lax.rem(r, 2)
    chip = lax.div(r, 2)
    y = lax.rem(chip, 4)
    x = lax.div(chip, 4)
    z = lax.rem(c, 4)
    far = lax.div(c, 4)
    up = (x * 8 + lax.rem(y + 1, 4) * 2 + core, c)
    down = (x * 8 + lax.rem(y + 3, 4) * 2 + core, c)
    across = ((1 - x) * 8 + y * 2 + core, c)
    pair = (chip * 2 + 1 - core, c)
    ahead = (r, far * 4 + lax.rem(z + 1, 4))
    behind = (r, far * 4 + lax.rem(z + 3, 4))
    over = (r, (1 - far) * 4 + z)

    barrier = pltpu.get_barrier_semaphore()
    for peer in (up, down, across, pair, ahead, behind, over):
        pl.semaphore_signal(barrier, inc=1, device_id=peer, device_id_type=MESH)
    pl.semaphore_wait(barrier, 7)

    def loop(first, last, act):
        lax.fori_loop(first, last, lambda i, carry: (act(i), carry)[1], 0)

    def pick(values, at):
        return sum(jnp.where(at == i, v, 0) for i, v in enumerate(values) if v)

    start = lambda copy: copy.start()
    sent = lambda copy: copy.wait_send()

    depth = tuple(pick(values, chip) for values in TREE_DEPTH)
    ways = tuple(tuple(pick(values, chip) == 1 for values in tree) for tree in TREE_WAYS)

    def wide_copy(j, way, target):
        rows = pl.ds(pl.multiple_of(lax.rem(j, PARTS) * CHUNK, CHUNK), CHUNK)
        chunk = panel.at[core, lax.div(j, PARTS), rows]
        return pltpu.make_async_remote_copy(
            src_ref=chunk,
            dst_ref=chunk,
            send_sem=wide_send.at[j, way],
            recv_sem=wide_recv.at[j],
            device_id=target,
            device_id_type=MESH,
        )

    def wide_each(tree, j, act):
        for way, target in enumerate((up, down, across)):

            @pl.when(ways[tree][way])
            def _():
                act(wide_copy(j, way, target))

    def wide_slot(first, end, slot, forward=False):
        for tree in range(3):
            j = 3 * (slot - SLOTS * depth[tree]) + tree

            @pl.when((j >= first) & (j < end))
            def _():
                wide_copy(j, 0, up).wait_recv()
                wide_each(tree, j, start)
                if forward:
                    last_copy(j).start()

    def wide_relay(first_block, end_block, forward=False):
        first, end = first_block * PARTS, end_block * PARTS
        loop(first // 3 - 1, (end + 2) // 3 + 4 * SLOTS, lambda slot: wide_slot(first, end, slot, forward))

    def wide_source(block, act):
        def one(j):
            for tree in range(3):

                @pl.when(lax.rem(j, 3) == tree)
                def _():
                    wide_each(tree, j, act)

        loop(block * PARTS, (block + 1) * PARTS, one)

    def pair_copy(b):
        block = panel.at[core, b]
        return pltpu.make_async_remote_copy(
            src_ref=block,
            dst_ref=block,
            send_sem=pair_send.at[b],
            recv_sem=pair_recv.at[b],
            device_id=pair,
            device_id_type=MESH,
        )

    def pair_wait(b):
        block = panel.at[1 - core, b]
        pltpu.make_async_remote_copy(
            src_ref=block,
            dst_ref=block,
            send_sem=pair_send.at[b],
            recv_sem=pair_recv.at[b],
            device_id=pair,
            device_id_type=MESH,
        ).wait_recv()

    def last_copy(j):
        rows = pl.ds(pl.multiple_of(lax.rem(j, PARTS) * CHUNK, CHUNK), CHUNK)
        chunk = panel.at[0, 3, rows]
        return pltpu.make_async_remote_copy(
            src_ref=chunk,
            dst_ref=chunk,
            send_sem=last_send.at[lax.rem(j, PARTS)],
            recv_sem=last_recv.at[lax.rem(j, PARTS)],
            device_id=pair,
            device_id_type=MESH,
        )

    def side_copy(s, j, way, target):
        chunk = side.at[s, pl.ds(pl.multiple_of(j * CHUNK, CHUNK), CHUNK)]
        return pltpu.make_async_remote_copy(
            src_ref=chunk,
            dst_ref=chunk,
            send_sem=side_send.at[s, j, way],
            recv_sem=side_recv.at[s, j],
            device_id=target,
            device_id_type=MESH,
        )

    places = tuple(far * 4 + lax.rem(z + 4 - s, 4) for s in range(2))
    side_depth = [[pick(values, place) for values in TREE_DEPTH] for place in places]
    side_ways = [
        [[pick(values, place) for values in tree] for tree in TREE_WAYS] for place in places
    ]

    def side_each(s, tree, j, act):
        for way, target in enumerate((ahead, behind, over)):

            @pl.when(side_ways[s][tree][way] == 1)
            def _():
                act(side_copy(s, j, way, target))

    def side_slot(slot):
        for s in range(2):
            for tree in range(3):
                j = 3 * (slot - 3 * s - SLOTS * side_depth[s][tree]) + tree

                @pl.when((j >= 0) & (j < PARTS))
                def _():
                    @pl.when(c != s)
                    def _():
                        side_copy(s, j, 0, ahead).wait_recv()

                    side_each(s, tree, j, start)

    SIDE_END = 6 + 4 * SLOTS

    def through_copy(b, j, way, target):
        chunk = panel.at[core, b, pl.ds(pl.multiple_of(j * CHUNK, CHUNK), CHUNK)]
        return pltpu.make_async_remote_copy(
            src_ref=chunk,
            dst_ref=chunk,
            send_sem=through_send.at[b - 2, j, way],
            recv_sem=through_recv.at[b - 2, j],
            device_id=target,
            device_id_type=MESH,
        )

    def through_each(b, s, tree, j, act):
        for way, target in enumerate((ahead, behind, over)):

            @pl.when(side_ways[s][tree][way] == 1)
            def _():
                act(through_copy(b, j, way, target))

    def through_slot(b, s, slot):
        for tree in range(3):
            j = 3 * (slot - SLOTS * side_depth[s][tree]) + tree

            @pl.when((j >= 0) & (j < PARTS))
            def _():
                @pl.when(c != s)
                def _():
                    through_copy(b, j, 0, ahead).wait_recv()

                through_each(b, s, tree, j, start)
                for kind in range(3):

                    @pl.when(lax.rem(b * PARTS + j, 3) == kind)
                    def _():
                        wide_each(kind, b * PARTS + j, start)

    THROUGH_END = (PARTS + 2) // 3 + 4 * SLOTS

    def through(b):
        loop(0, THROUGH_END, lambda slot: through_slot(b, 0, slot))

    def through_sent(b, s):
        def one(j):
            for tree in range(3):

                @pl.when(lax.rem(j, 3) == tree)
                def _():
                    through_each(b, s, tree, j, sent)

        loop(0, PARTS, one)

    def put(index, value):
        high, low = split(value)
        ph[index] = high
        pl_[index] = low

    def times(i, j):
        return product(ph[i], pl_[i], ph[j], pl_[j])

    def invert():
        here = lax.broadcasted_iota(jnp.int32, (B, B), 0) == lax.broadcasted_iota(jnp.int32, (B, B), 1)
        block = pivot[...]
        only = jnp.where(here, block, 0.0)
        one_row = 1.0 / jnp.sum(only, axis=0, keepdims=True)
        one_col = 1.0 / jnp.sum(only, axis=1, keepdims=True)
        eye = jnp.where(here, 1.0, 0.0)
        rest = eye - block * one_row
        xf[...] = one_col * (eye + rest)
        high, low = split(rest)
        sh[0, B:] = high
        sl[0, B:] = low
        high, low = split(product(sh[0, B:], sl[0, B:], sh[0, B:], sl[0, B:]))
        sh[1, B:] = high
        sl[1, B:] = low
        high, low = split(xf[...])
        sh[1, :B] = high
        sl[1, :B] = low

        def step(k):
            now = lax.rem(k, 2)
            later = 1 - now
            both = product(sh[now], sl[now], sh[now, B:], sl[now, B:])
            total = xf[...] + both[:B]
            xf[...] = total
            high, low = split(total)
            sh[later, :B] = high
            sl[later, :B] = low
            high, low = split(both[B:])
            sh[later, B:] = high
            sl[later, B:] = low

        loop(1, NS_STEPS - 1, step)
        now = (NS_STEPS - 1) % 2
        return xf[...] + product(sh[now, :B], sl[now, :B], sh[now, B:], sl[now, B:])

    def direct_copy(src, dst, at, target):
        return pltpu.make_async_remote_copy(
            src_ref=src,
            dst_ref=dst,
            send_sem=direct_send.at[at],
            recv_sem=direct_recv.at[at],
            device_id=target,
            device_id_type=MESH,
        )

    first_copy = direct_copy(a_ref.at[0], direct.at[0], 0, behind)
    second_copy = direct_copy(direct.at[1], direct.at[1], 1, behind)
    corner_copy = direct_copy(a_ref.at[0], direct.at[1], 2, pair)
    cross_copy = direct_copy(a_ref.at[0], panel.at[1, 3], 3, pair)

    @pl.when((r == 1) & (c == 1))
    def _():
        corner_copy.start()

    @pl.when((r == 0) & (c == 1))
    def _():
        cross_copy.start()
        first_copy.start()
        corner_copy.wait_recv()
        second_copy.start()

    @pl.when((r == 1) & (c == 0))
    def _():
        panel[1, 2] = a_ref[0]
        pair_copy(2).start()

    @pl.when(r < 2)
    def _():
        panel[core, 0] = a_ref[0]
        panel[core, 1] = a_ref[1]

        @pl.when(r == 0)
        def _():
            pair_copy(0).start()
            pair_copy(1).start()

        wide_source(0, start)
        wide_source(1, start)

    @pl.when((r == 0) & (c == 0))
    def _():
        pivot[...] = a_ref[0]
        first = invert()
        panel[0, 2] = first
        through(2)
        pair_copy(2).start()
        put(0, first)
        first_copy.wait_recv()
        put(1, direct[0])
        put(2, times(0, 1))
        pair_wait(2)
        put(3, panel[1, 2])
        second_copy.wait_recv()
        pivot[...] = direct[1] - times(3, 2)
        panel[0, 3] = invert()
        through(3)
        loop(0, PARTS, lambda j: last_copy(j).start())

    @pl.when((r == 0) & (c != 0))
    def _():
        through(2)
        pair_copy(2).start()
        through(3)
        loop(0, PARTS, lambda j: last_copy(j).start())

    @pl.when(r == 0)
    def _():
        put(0, panel[0, 2])
        for j in range(2):
            put(1, a_ref[j])
            out_ref[j] = times(0, 1)

    @pl.when(r == 1)
    def _():
        @pl.when(c == 1)
        def _():
            cross_copy.wait_recv()

        def both(slot):
            through_slot(2, 0, slot)
            through_slot(3, 1, slot - 1)

        loop(0, THROUGH_END + 1, both)
        put(3, panel[1, 2])

    @pl.when(r >= 2)
    def _():
        for s in range(2):

            @pl.when(c == s)
            def _():
                side[s] = a_ref[0]

        def early(slot):
            side_slot(slot)
            wide_slot(0, 2 * PARTS, slot)

        loop(0, SIDE_END, early)
        pair_copy(0).start()
        pair_copy(1).start()
        put(3, side[0])

    @pl.when((r >= 2) & (core == 0))
    def _():
        wide_relay(2, 3)
        pair_copy(2).start()
        for b in range(3):
            pair_wait(b)

    @pl.when((r >= 2) & (core == 1))
    def _():
        wide_relay(2, 4)
        pair_copy(2).start()
        pair_copy(3).start()

    @pl.when(core == 1)
    def _():
        for b in range(3):
            pair_wait(b)

    @pl.when(r >= 1)
    def _():
        put(0, panel[0, 2])
        for j in range(2):
            put(1, panel[0, j])
            put(4 + j, times(0, 1))
            kept = a_ref[j] - times(3, 4 + j)
            out_ref[j] = kept

            @pl.when(r == 1)
            def _():
                put(6 + j, kept)

        @pl.when(r >= 2)
        def _():
            put(1, panel[1, 2])
            for j in range(2):
                put(6 + j, panel[1, j] - times(1, 4 + j))

            @pl.when(core == 0)
            def _():
                pair_wait(3)

            put(1, panel[1, 3])
            put(2, times(0, 1))
            put(4, side[1] - times(3, 2))

        @pl.when((r >= 2) & (core == 0))
        def _():
            wide_relay(3, 4, forward=True)

        @pl.when(core == 1)
        def _():
            loop(0, PARTS, lambda j: last_copy(j).wait_recv())

        put(0, panel[0, 3])

        @pl.when(r >= 2)
        def _():
            put(0, times(4, 0))

        for j in range(2):
            scaled = times(0, 6 + j)
            live = c >= 2 if j == 0 else c >= 0

            @pl.when((r == 1) & live)
            def _():
                out_ref[j] = scaled

            @pl.when((r >= 2) & live)
            def _():
                out_ref[j] = out_ref[j] - scaled

    @pl.when(c == 0)
    def _():
        out_ref[0] = a_ref[0]

    for b in range(4):
        wide_source(b, sent)

    @pl.when(r < 2)
    def _():
        through_sent(2, 0)

    @pl.when(r == 0)
    def _():
        through_sent(3, 0)

        @pl.when(c == 1)
        def _():
            cross_copy.wait_send()
            first_copy.wait_send()
            second_copy.wait_send()

    @pl.when(r == 1)
    def _():
        through_sent(3, 1)

        @pl.when(c == 0)
        def _():
            pair_copy(2).wait_send()

        @pl.when(c == 1)
        def _():
            corner_copy.wait_send()

    @pl.when(core == 0)
    def _():
        for b in range(3):
            pair_copy(b).wait_send()
        loop(0, PARTS, lambda j: last_copy(j).wait_send())

    @pl.when(r >= 2)
    def _():
        @pl.when(core == 1)
        def _():
            for b in range(4):
                pair_copy(b).wait_send()

        for s in range(2):

            def one(j):
                for tree in range(3):

                    @pl.when(lax.rem(j, 3) == tree)
                    def _():
                        side_each(s, tree, j, sent)

            loop(0, PARTS, one)


def eliminate(blocks):
    vmem = pl.BlockSpec(memory_space=pltpu.VMEM)
    dma = pltpu.SemaphoreType.DMA
    return pl.pallas_call(
        eliminate_kernel,
        out_shape=jax.ShapeDtypeStruct((2, B, B), F32),
        in_specs=[vmem],
        out_specs=vmem,
        scratch_shapes=[
            pltpu.VMEM((2, B, B), F32),
            pltpu.VMEM((2, 4, B, B), F32),
            pltpu.VMEM((2, B, B), F32),
            pltpu.VMEM((B, B), F32),
            pltpu.VMEM((8, B, B), BF16),
            pltpu.VMEM((8, B, B), BF16),
            pltpu.VMEM((2, 2 * B, B), BF16),
            pltpu.VMEM((2, 2 * B, B), BF16),
            pltpu.VMEM((B, B), F32),
            dma((4 * PARTS, 3)),
            dma((4 * PARTS,)),
            dma((4,)),
            dma((4,)),
            dma((2, PARTS, 3)),
            dma((2, PARTS)),
            dma((4,)),
            dma((4,)),
            dma((2, PARTS, 3)),
            dma((2, PARTS)),
            dma((PARTS,)),
            dma((PARTS,)),
        ],
        compiler_params=pltpu.CompilerParams(
            collective_id=1, has_side_effects=True, vmem_limit_bytes=VMEM_LIMIT
        ),
        name="eliminate",
    )(blocks)


def per_device(base, block_mask, heads, coef, weir_node, weir_cell):
    blocks = base.reshape(2, B, B)
    every_head = gather_heads(heads)
    blocks = add_weirs(blocks, block_mask, every_head, coef, weir_node, weir_cell)
    return eliminate(blocks).reshape(base.shape)


def solution(mesh):
    placed = (P(None, "wide", None, "narrow", None, None), P(), P("narrow"), P(), P(), P())
    return jax.shard_map(
        per_device,
        mesh=mesh,
        in_specs=placed,
        out_specs=P(None, "wide", None, "narrow", None, None),
        check_vma=False,
    )
```

```python
import functools

import jax
import jax.numpy as jnp
from jax import lax
from jax.experimental import pallas as pl
from jax.experimental.pallas import tpu as pltpu
from jax.sharding import PartitionSpec as P

NS_STEPS = 6
B = 512
ROWS = 72
LANES = 128
MESH = pl.DeviceIdType.MESH
F32 = jnp.float32
BF16 = jnp.bfloat16
VMEM_LIMIT = 56 * 2**20
SLOTS = 2
CHUNK = 64
PARTS = B // CHUNK
TREE_DEPTH = ((0, 1, 2, 3, 3, 2, 3, 4), (0, 3, 2, 1, 3, 4, 3, 2), (0, 3, 4, 3, 1, 2, 3, 2))
TREE_WAYS = (
    ((1, 1, 1, 0, 0, 0, 1, 0), (0, 0, 0, 0, 0, 1, 0, 0), (0, 1, 1, 0, 0, 0, 0, 0)),
    ((0, 0, 0, 0, 0, 0, 0, 1), (1, 0, 1, 1, 0, 0, 1, 1), (0, 0, 0, 1, 0, 0, 0, 0)),
    ((0, 0, 0, 0, 1, 1, 0, 0), (0, 0, 0, 0, 1, 0, 0, 0), (1, 0, 0, 0, 0, 1, 1, 1)),
)


def split(x):
    high = x.astype(BF16)
    return high, (x - high.astype(F32)).astype(BF16)


def dot(a, b):
    return jnp.dot(a, b, preferred_element_type=F32)


def dot_nt(a, b):
    return lax.dot_general(a, b, (((1,), (1,)), ((), ())), preferred_element_type=F32)


def product(ah, al, bh, bl):
    return dot(ah, bh) + dot(ah, bl) + dot(al, bh)


def lookup(table_ref, first, index):
    high = lax.shift_right_logical(index, 7) - first
    low = jnp.bitwise_and(index, 127)
    found = jnp.zeros(index.shape, F32)
    for t in range(32):
        row = jnp.broadcast_to(table_ref[pl.ds(first + t, 1), :], index.shape)
        picked = jnp.take_along_axis(row, low, axis=1, mode="promise_in_bounds")
        found = jnp.where(high == t, picked, found)
    return found


def pieces(x):
    high = x.astype(BF16).astype(F32)
    rest = x - high
    middle = rest.astype(BF16).astype(F32)
    return high, middle, rest - middle


def solve_kernel(
    mask_ref,
    base_ref,
    heads_ref,
    coef_ref,
    node_ref,
    cell_ref,
    out_ref,
    own,
    every,
    row_of,
    col_of,
    flux_high,
    flux_low,
    diagonal,
    side,
    panel,
    direct,
    pivot,
    ph,
    pl_,
    sh,
    sl,
    xf,
    wide_send,
    wide_recv,
    pair_send,
    pair_recv,
    side_send,
    side_recv,
    direct_send,
    direct_recv,
    through_send,
    through_recv,
    last_send,
    last_recv,
    heads_send,
    heads_recv,
):
    r = lax.axis_index("wide")
    c = lax.axis_index("narrow")
    core = lax.rem(r, 2)
    chip = lax.div(r, 2)
    y = lax.rem(chip, 4)
    x = lax.div(chip, 4)
    z = lax.rem(c, 4)
    far = lax.div(c, 4)
    up = (x * 8 + lax.rem(y + 1, 4) * 2 + core, c)
    down = (x * 8 + lax.rem(y + 3, 4) * 2 + core, c)
    across = ((1 - x) * 8 + y * 2 + core, c)
    pair = (chip * 2 + 1 - core, c)
    ahead = (r, far * 4 + lax.rem(z + 1, 4))
    behind = (r, far * 4 + lax.rem(z + 3, 4))
    over = (r, (1 - far) * 4 + z)

    barrier = pltpu.get_barrier_semaphore()
    for peer in (up, down, across, pair):
        pl.semaphore_signal(barrier, inc=1, device_id=peer, device_id_type=MESH)
    for hop in range(1, 8):
        pl.semaphore_signal(barrier, inc=1, device_id=(r, lax.rem(c + hop, 8)), device_id_type=MESH)
    pl.semaphore_wait(barrier, 11)

    def loop(first, last, act):
        lax.fori_loop(first, last, lambda i, carry: (act(i), carry)[1], 0)

    def pick(values, at):
        return sum(jnp.where(at == i, v, 0) for i, v in enumerate(values) if v)

    start = lambda copy: copy.start()
    sent = lambda copy: copy.wait_send()

    depth = tuple(pick(values, chip) for values in TREE_DEPTH)
    ways = tuple(tuple(pick(values, chip) == 1 for values in tree) for tree in TREE_WAYS)

    def wide_copy(j, way, target):
        rows = pl.ds(pl.multiple_of(lax.rem(j, PARTS) * CHUNK, CHUNK), CHUNK)
        chunk = panel.at[core, lax.div(j, PARTS), rows]
        return pltpu.make_async_remote_copy(
            src_ref=chunk,
            dst_ref=chunk,
            send_sem=wide_send.at[j, way],
            recv_sem=wide_recv.at[j],
            device_id=target,
            device_id_type=MESH,
        )

    def wide_each(tree, j, act):
        for way, target in enumerate((up, down, across)):

            @pl.when(ways[tree][way])
            def _():
                act(wide_copy(j, way, target))

    def wide_slot(first, end, slot, forward=False):
        for tree in range(3):
            j = 3 * (slot - SLOTS * depth[tree]) + tree

            @pl.when((j >= first) & (j < end))
            def _():
                wide_copy(j, 0, up).wait_recv()
                wide_each(tree, j, start)
                if forward:
                    last_copy(j).start()

    def wide_relay(first_block, end_block, forward=False):
        first, end = first_block * PARTS, end_block * PARTS
        loop(first // 3 - 1, (end + 2) // 3 + 4 * SLOTS, lambda slot: wide_slot(first, end, slot, forward))

    def wide_source(block, act):
        def one(j):
            for tree in range(3):

                @pl.when(lax.rem(j, 3) == tree)
                def _():
                    wide_each(tree, j, act)

        loop(block * PARTS, (block + 1) * PARTS, one)

    def pair_copy(b):
        block = panel.at[core, b]
        return pltpu.make_async_remote_copy(
            src_ref=block,
            dst_ref=block,
            send_sem=pair_send.at[b],
            recv_sem=pair_recv.at[b],
            device_id=pair,
            device_id_type=MESH,
        )

    def pair_wait(b):
        block = panel.at[1 - core, b]
        pltpu.make_async_remote_copy(
            src_ref=block,
            dst_ref=block,
            send_sem=pair_send.at[b],
            recv_sem=pair_recv.at[b],
            device_id=pair,
            device_id_type=MESH,
        ).wait_recv()

    def last_copy(j):
        rows = pl.ds(pl.multiple_of(lax.rem(j, PARTS) * CHUNK, CHUNK), CHUNK)
        chunk = panel.at[0, 3, rows]
        return pltpu.make_async_remote_copy(
            src_ref=chunk,
            dst_ref=chunk,
            send_sem=last_send.at[lax.rem(j, PARTS)],
            recv_sem=last_recv.at[lax.rem(j, PARTS)],
            device_id=pair,
            device_id_type=MESH,
        )

    def side_copy(s, j, way, target):
        chunk = side.at[s, pl.ds(pl.multiple_of(j * CHUNK, CHUNK), CHUNK)]
        return pltpu.make_async_remote_copy(
            src_ref=chunk,
            dst_ref=chunk,
            send_sem=side_send.at[s, j, way],
            recv_sem=side_recv.at[s, j],
            device_id=target,
            device_id_type=MESH,
        )

    places = tuple(far * 4 + lax.rem(z + 4 - s, 4) for s in range(2))
    side_depth = [[pick(values, place) for values in TREE_DEPTH] for place in places]
    side_ways = [
        [[pick(values, place) for values in tree] for tree in TREE_WAYS] for place in places
    ]

    def side_each(s, tree, j, act):
        for way, target in enumerate((ahead, behind, over)):

            @pl.when(side_ways[s][tree][way] == 1)
            def _():
                act(side_copy(s, j, way, target))

    def side_slot(slot):
        for s in range(2):
            for tree in range(3):
                j = 3 * (slot - 3 * s - SLOTS * side_depth[s][tree]) + tree

                @pl.when((j >= 0) & (j < PARTS))
                def _():
                    @pl.when(c != s)
                    def _():
                        side_copy(s, j, 0, ahead).wait_recv()

                    side_each(s, tree, j, start)

    SIDE_END = 6 + 4 * SLOTS

    def through_copy(b, j, way, target):
        chunk = panel.at[core, b, pl.ds(pl.multiple_of(j * CHUNK, CHUNK), CHUNK)]
        return pltpu.make_async_remote_copy(
            src_ref=chunk,
            dst_ref=chunk,
            send_sem=through_send.at[b - 2, j, way],
            recv_sem=through_recv.at[b - 2, j],
            device_id=target,
            device_id_type=MESH,
        )

    def through_each(b, s, tree, j, act):
        for way, target in enumerate((ahead, behind, over)):

            @pl.when(side_ways[s][tree][way] == 1)
            def _():
                act(through_copy(b, j, way, target))

    def through_slot(b, s, slot):
        for tree in range(3):
            j = 3 * (slot - SLOTS * side_depth[s][tree]) + tree

            @pl.when((j >= 0) & (j < PARTS))
            def _():
                @pl.when(c != s)
                def _():
                    through_copy(b, j, 0, ahead).wait_recv()

                through_each(b, s, tree, j, start)
                for kind in range(3):

                    @pl.when(lax.rem(b * PARTS + j, 3) == kind)
                    def _():
                        wide_each(kind, b * PARTS + j, start)

    THROUGH_END = (PARTS + 2) // 3 + 4 * SLOTS

    def through(b):
        loop(0, THROUGH_END, lambda slot: through_slot(b, 0, slot))

    def through_sent(b, s):
        def one(j):
            for tree in range(3):

                @pl.when(lax.rem(j, 3) == tree)
                def _():
                    through_each(b, s, tree, j, sent)

        loop(0, PARTS, one)

    def put(index, value):
        high, low = split(value)
        ph[index] = high
        pl_[index] = low

    def times(i, j):
        return product(ph[i], pl_[i], ph[j], pl_[j])

    def invert():
        here = lax.broadcasted_iota(jnp.int32, (B, B), 0) == lax.broadcasted_iota(jnp.int32, (B, B), 1)
        block = pivot[...]
        only = jnp.where(here, block, 0.0)
        one_row = 1.0 / jnp.sum(only, axis=0, keepdims=True)
        one_col = 1.0 / jnp.sum(only, axis=1, keepdims=True)
        eye = jnp.where(here, 1.0, 0.0)
        rest = eye - block * one_row
        xf[...] = one_col * (eye + rest)
        high, low = split(rest)
        sh[0, B:] = high
        sl[0, B:] = low
        high, low = split(product(sh[0, B:], sl[0, B:], sh[0, B:], sl[0, B:]))
        sh[1, B:] = high
        sl[1, B:] = low
        high, low = split(xf[...])
        sh[1, :B] = high
        sl[1, :B] = low

        def step(k):
            now = lax.rem(k, 2)
            later = 1 - now
            both = product(sh[now], sl[now], sh[now, B:], sl[now, B:])
            total = xf[...] + both[:B]
            xf[...] = total
            high, low = split(total)
            sh[later, :B] = high
            sl[later, :B] = low
            high, low = split(both[B:])
            sh[later, B:] = high
            sl[later, B:] = low

        loop(1, NS_STEPS - 1, step)
        now = (NS_STEPS - 1) % 2
        return xf[...] + product(sh[now, :B], sl[now, :B], sh[now, B:], sl[now, B:])

    def direct_copy(src, dst, at, target):
        return pltpu.make_async_remote_copy(
            src_ref=src,
            dst_ref=dst,
            send_sem=direct_send.at[at],
            recv_sem=direct_recv.at[at],
            device_id=target,
            device_id_type=MESH,
        )

    raw = panel.at[core, 0]
    first_copy = direct_copy(raw, direct.at[0], 0, behind)
    second_copy = direct_copy(direct.at[1], direct.at[1], 1, behind)
    corner_copy = direct_copy(raw, direct.at[1], 2, pair)
    cross_copy = direct_copy(raw, panel.at[1, 3], 3, pair)

    def heads_copy(hop):
        return pltpu.make_async_remote_copy(
            src_ref=heads_ref,
            dst_ref=every.at[pl.ds(pl.multiple_of(c * 8, 8), 8)],
            send_sem=heads_send.at[hop],
            recv_sem=heads_recv.at[hop],
            device_id=(r, lax.rem(c + hop, 8)),
            device_id_type=MESH,
        )

    loop(1, 8, lambda hop: heads_copy(hop).start())
    every[pl.ds(pl.multiple_of(c * 8, 8), 8)] = heads_ref[...]

    for j in range(2):
        col = c + 8 * j
        keep = jnp.where((mask_ref[r, col] != 0) | (r == col), 1.0, 0.0).astype(F32)
        own[j] = base_ref[j] * keep

    @pl.when(r < 2)
    def _():
        panel[core, 0] = own[0]

        @pl.when((r == 1) & (c == 1))
        def _():
            corner_copy.start()

        @pl.when((r == 0) & (c == 1))
        def _():
            cross_copy.start()
            first_copy.start()

        @pl.when((r == 1) & (c == 0))
        def _():
            panel[1, 2] = own[0]
            pair_copy(2).start()

        @pl.when(r == 0)
        def _():
            pair_copy(0).start()

        wide_source(0, start)

    for s in range(2):

        @pl.when((r >= 2) & (r < 8) & (c == s))
        def _():
            side[s] = own[0]

    loop(1, 8, lambda hop: heads_copy(hop).wait_recv())
    upper = r < 8
    node = node_ref[...]
    cell = cell_ref[...]
    drop = lookup(every, 0, node) - lookup(every, 32, cell)
    flux = 1.5 * coef_ref[...] * jnp.sqrt(drop * drop + 0.01)
    weir_row = jnp.where(upper, node, cell)
    weir_col = jnp.where(upper, cell, node)
    hit = (lax.shift_right_logical(weir_row, 9) == r) & (
        lax.shift_right_logical(weir_col, 9) == jnp.where(upper, c + 8, c)
    )
    row_of[...] = jnp.bitwise_and(weir_row, 511)
    col_of[...] = jnp.bitwise_and(weir_col, 511)
    high, middle, low = pieces(flux)
    flux_high[...] = jnp.where(hit, high, 0.0)
    flux_low[...] = jnp.where(hit, flux - high, 0.0)
    slot_of = jnp.where(upper, 1, 0)

    def add_diagonal(ref, at, first):
        here = lax.broadcasted_iota(jnp.int32, (LANES, LANES), 0)
        eye = here == lax.broadcasted_iota(jnp.int32, (LANES, LANES), 1)
        for t in range(4):
            part = pl.ds(t * LANES, LANES)
            ref[at, part, part] = ref[at, part, part] + jnp.where(eye, diagonal[first + t : first + t + 1], 0.0)

    @pl.when(c == lax.rem(r, 8))
    def _():
        strip = lax.shift_right_logical(weir_row, 7) - 4 * r
        lane = jnp.bitwise_and(weir_row, 127)
        here8 = lax.broadcasted_iota(jnp.int32, (8, LANES), 0)
        here128 = lax.broadcasted_iota(jnp.int32, (LANES, LANES), 0)
        total = jnp.zeros((24, LANES), F32)
        for g in range(ROWS // 8):
            ones = []
            lefts = []
            for t in range(8 * g, 8 * g + 8):
                ones.append(jnp.where(here128 == lane[t : t + 1], 1.0, 0.0).astype(BF16))
                at = here8 == strip[t : t + 1]
                lefts.append(
                    jnp.concatenate(
                        [jnp.where(at, part[t : t + 1], 0.0) for part in (high, middle, low)], axis=0
                    ).astype(BF16)
                )
            total = total + dot_nt(jnp.concatenate(lefts, axis=1), jnp.concatenate(ones, axis=1))
        diagonal[...] = total[0:8] + total[8:16] + total[16:24]
        add_diagonal(own, jnp.where(upper, 0, 1), 0)

    def scatter(b):
        rows = pl.ds(pl.multiple_of(b * 8, 8), 8)
        here = lax.broadcasted_iota(jnp.int32, (B, LANES), 0)
        at_row = row_of[rows]
        at_col = col_of[rows]
        right = jnp.concatenate(
            [jnp.where(here == at_col[t : t + 1], 1.0, 0.0).astype(BF16) for t in range(8)], axis=1
        )
        total = jnp.zeros((B, B), F32)
        for part in (flux_high[rows], flux_low[rows]):
            left = jnp.concatenate(
                [jnp.where(here == at_row[t : t + 1], part[t : t + 1], 0.0).astype(BF16) for t in range(8)],
                axis=1,
            )
            total = total + dot_nt(left, right)
        own[slot_of] = own[slot_of] - total

    STEPS = ROWS // 8
    LATER = (STEPS + 1) // 2

    def second_block():
        panel[core, 1] = own[1]

        @pl.when(r == 0)
        def _():
            pair_copy(1).start()

        wide_source(1, start)

    @pl.when((r == 0) & (c == 1))
    def _():
        corner_copy.wait_recv()
        second_copy.start()

    @pl.when((r == 0) & (c == 0))
    def _():
        pivot[...] = own[0]
        first = invert()
        panel[0, 2] = first
        through(2)
        pair_copy(2).start()
        put(0, first)
        loop(0, STEPS, scatter)
        second_block()
        first_copy.wait_recv()
        put(1, direct[0])
        put(2, times(0, 1))
        pair_wait(2)
        put(3, panel[1, 2])
        second_copy.wait_recv()
        add_diagonal(direct, 1, 4)
        pivot[...] = direct[1] - times(3, 2)
        panel[0, 3] = invert()
        through(3)
        loop(0, PARTS, lambda j: last_copy(j).start())

    @pl.when((r == 0) & (c != 0))
    def _():
        loop(0, STEPS, scatter)
        second_block()
        through(2)
        pair_copy(2).start()
        through(3)
        loop(0, PARTS, lambda j: last_copy(j).start())

    @pl.when(r == 0)
    def _():
        put(0, panel[0, 2])
        for j in range(2):
            put(1, own[j])
            out_ref[j] = times(0, 1)

    @pl.when(r == 1)
    def _():
        @pl.when(c == 1)
        def _():
            cross_copy.wait_recv()

        def both(slot):
            through_slot(2, 0, slot)
            through_slot(3, 1, slot - 3)

        loop(0, STEPS, scatter)
        second_block()
        loop(0, THROUGH_END + 3, both)
        put(3, panel[1, 2])

    @pl.when(r >= 2)
    def _():
        end = jnp.where(core == 0, 3 * PARTS, 4 * PARTS)
        behind_by = jnp.where(upper, 0, LATER)

        def early(slot):
            wide_slot(0, end, slot)
            side_slot(slot - behind_by)
            for b in range(3):

                @pl.when(slot == (b * PARTS + PARTS - 1) // 3 + 4 * SLOTS)
                def _():
                    pair_copy(b).start()

        def step(slot):
            scatter(2 * slot)

            @pl.when(2 * slot + 1 < STEPS)
            def _():
                scatter(2 * slot + 1)

            early(slot)

        loop(0, LATER, step)
        for s in range(2):

            @pl.when((r >= 8) & (c == s))
            def _():
                side[s] = own[0]

        loop(LATER, SIDE_END + LATER + 1, early)

        @pl.when(core == 1)
        def _():
            pair_copy(3).start()

        put(3, side[0])

        @pl.when(core == 0)
        def _():
            for b in range(3):
                pair_wait(b)

    @pl.when(core == 1)
    def _():
        for b in range(3):
            pair_wait(b)

    last_first = jnp.where((core == 0) & (r >= 2), 3 * PARTS, 4 * PARTS)

    def last_slot(slot):
        wide_slot(last_first, 4 * PARTS, slot, forward=True)

    def scaled_row(j):
        put(1, panel[0, j])
        put(4 + j, times(0, 1))

    def kept_row(j):
        kept = own[j] - times(3, 4 + j)
        out_ref[j] = kept

        @pl.when(r == 1)
        def _():
            put(6 + j, kept)

    def first_rest(j):
        @pl.when(r >= 2)
        def _():
            if j == 0:
                put(1, panel[1, 2])
            put(6 + j, panel[1, j] - times(1, 4 + j))

    def corner_row():
        @pl.when(r >= 2)
        def _():
            @pl.when(core == 0)
            def _():
                pair_wait(3)

            put(1, panel[1, 3])
            put(2, times(0, 1))

    def column():
        @pl.when(r >= 2)
        def _():
            put(4, side[1] - times(3, 2))

    @pl.when(r >= 1)
    def _():
        put(0, panel[0, 2])
        work = [
            lambda: scaled_row(0),
            lambda: scaled_row(1),
            lambda: kept_row(0),
            lambda: kept_row(1),
            lambda: first_rest(0),
            lambda: first_rest(1),
            corner_row,
            column,
        ]
        base = 3 * PARTS // 3
        slots = list(range(base, base + 3 + 4 * SLOTS + 1))
        for k, slot in enumerate(slots):
            last_slot(slot)
            if k < len(work):
                work[k]()

        @pl.when(core == 1)
        def _():
            loop(0, PARTS, lambda j: last_copy(j).wait_recv())

        put(0, panel[0, 3])

        @pl.when(r >= 2)
        def _():
            put(0, times(4, 0))

        for j in range(2):
            scaled = times(0, 6 + j)
            live = c >= 2 if j == 0 else c >= 0

            @pl.when((r == 1) & live)
            def _():
                out_ref[j] = scaled

            @pl.when((r >= 2) & live)
            def _():
                out_ref[j] = out_ref[j] - scaled

    @pl.when(c == 0)
    def _():
        out_ref[0] = own[0]

    loop(1, 8, lambda hop: heads_copy(hop).wait_send())
    for b in range(4):
        wide_source(b, sent)

    @pl.when(r < 2)
    def _():
        through_sent(2, 0)

    @pl.when(r == 0)
    def _():
        through_sent(3, 0)

        @pl.when(c == 1)
        def _():
            cross_copy.wait_send()
            first_copy.wait_send()
            second_copy.wait_send()

    @pl.when(r == 1)
    def _():
        through_sent(3, 1)

        @pl.when(c == 0)
        def _():
            pair_copy(2).wait_send()

        @pl.when(c == 1)
        def _():
            corner_copy.wait_send()

    @pl.when(core == 0)
    def _():
        for b in range(3):
            pair_copy(b).wait_send()
        loop(0, PARTS, lambda j: last_copy(j).wait_send())

    @pl.when(r >= 2)
    def _():
        @pl.when(core == 1)
        def _():
            for b in range(4):
                pair_copy(b).wait_send()

        for s in range(2):

            def one(j):
                for tree in range(3):

                    @pl.when(lax.rem(j, 3) == tree)
                    def _():
                        side_each(s, tree, j, sent)

            loop(0, PARTS, one)


def per_device(base, block_mask, heads, coef, weir_node, weir_cell):
    pad = ROWS * LANES - coef.shape[0]
    coef = jnp.pad(coef, (0, pad)).reshape(ROWS, LANES)
    node = jnp.pad(weir_node, (0, pad)).reshape(ROWS, LANES)
    cell = jnp.pad(weir_cell, (0, pad), constant_values=4096).reshape(ROWS, LANES)
    vmem = pl.BlockSpec(memory_space=pltpu.VMEM)
    dma = pltpu.SemaphoreType.DMA
    weirs = (ROWS, LANES)
    out = pl.pallas_call(
        solve_kernel,
        out_shape=jax.ShapeDtypeStruct((2, B, B), F32),
        in_specs=[pl.BlockSpec(memory_space=pltpu.SMEM)] + [vmem] * 5,
        out_specs=vmem,
        scratch_shapes=[
            pltpu.VMEM((2, B, B), F32),
            pltpu.VMEM((64, LANES), F32),
            pltpu.VMEM(weirs, jnp.int32),
            pltpu.VMEM(weirs, jnp.int32),
            pltpu.VMEM(weirs, F32),
            pltpu.VMEM(weirs, F32),
            pltpu.VMEM((8, LANES), F32),
            pltpu.VMEM((2, B, B), F32),
            pltpu.VMEM((2, 4, B, B), F32),
            pltpu.VMEM((2, B, B), F32),
            pltpu.VMEM((B, B), F32),
            pltpu.VMEM((8, B, B), BF16),
            pltpu.VMEM((8, B, B), BF16),
            pltpu.VMEM((2, 2 * B, B), BF16),
            pltpu.VMEM((2, 2 * B, B), BF16),
            pltpu.VMEM((B, B), F32),
            dma((4 * PARTS, 3)),
            dma((4 * PARTS,)),
            dma((4,)),
            dma((4,)),
            dma((2, PARTS, 3)),
            dma((2, PARTS)),
            dma((4,)),
            dma((4,)),
            dma((2, PARTS, 3)),
            dma((2, PARTS)),
            dma((PARTS,)),
            dma((PARTS,)),
            dma((8,)),
            dma((8,)),
        ],
        compiler_params=pltpu.CompilerParams(
            collective_id=0, has_side_effects=True, vmem_limit_bytes=VMEM_LIMIT
        ),
        name="solve",
    )(block_mask, base.reshape(2, B, B), heads.reshape(8, LANES), coef, node, cell)
    return out.reshape(base.shape)


def solution(mesh):
    placed = (P(None, "wide", None, "narrow", None, None), P(), P("narrow"), P(), P(), P())
    return jax.shard_map(
        per_device,
        mesh=mesh,
        in_specs=placed,
        out_specs=P(None, "wide", None, "narrow", None, None),
        check_vma=False,
    )
```

```python
import functools

import jax
import jax.numpy as jnp
from jax import lax
from jax.experimental import pallas as pl
from jax.experimental.pallas import tpu as pltpu
from jax.sharding import PartitionSpec as P

NS_STEPS = 6
B = 512
ROWS = 72
LANES = 128
MESH = pl.DeviceIdType.MESH
F32 = jnp.float32
BF16 = jnp.bfloat16
VMEM_LIMIT = 56 * 2**20
SLOTS = 2
CHUNK = 64
PARTS = B // CHUNK
TREE_DEPTH = ((0, 1, 2, 3, 3, 2, 3, 4), (0, 3, 2, 1, 3, 4, 3, 2), (0, 3, 4, 3, 1, 2, 3, 2))
TREE_WAYS = (
    ((1, 1, 1, 0, 0, 0, 1, 0), (0, 0, 0, 0, 0, 1, 0, 0), (0, 1, 1, 0, 0, 0, 0, 0)),
    ((0, 0, 0, 0, 0, 0, 0, 1), (1, 0, 1, 1, 0, 0, 1, 1), (0, 0, 0, 1, 0, 0, 0, 0)),
    ((0, 0, 0, 0, 1, 1, 0, 0), (0, 0, 0, 0, 1, 0, 0, 0), (1, 0, 0, 0, 0, 1, 1, 1)),
)


def split(x):
    high = x.astype(BF16)
    return high, (x - high.astype(F32)).astype(BF16)


def dot(a, b):
    return jnp.dot(a, b, preferred_element_type=F32)


def dot_nt(a, b):
    return lax.dot_general(a, b, (((1,), (1,)), ((), ())), preferred_element_type=F32)


def product(ah, al, bh, bl):
    return dot(ah, bh) + dot(ah, bl) + dot(al, bh)


def gather_heads_kernel(mine_ref, every_ref, send_sem, recv_sem):
    r = lax.axis_index("wide")
    c = lax.axis_index("narrow")
    count = 8
    barrier = pltpu.get_barrier_semaphore()
    for hop in range(1, count):
        pl.semaphore_signal(barrier, inc=1, device_id=(r, lax.rem(c + hop, count)), device_id_type=MESH)
    pl.semaphore_wait(barrier, count - 1)
    place = pl.ds(pl.multiple_of(c * 8, 8), 8)
    copies = []
    for hop in range(1, count):
        copy = pltpu.make_async_remote_copy(
            src_ref=mine_ref,
            dst_ref=every_ref.at[place],
            send_sem=send_sem.at[hop],
            recv_sem=recv_sem.at[hop],
            device_id=(r, lax.rem(c + hop, count)),
            device_id_type=MESH,
        )
        copy.start()
        copies.append(copy)
    every_ref[place] = mine_ref[...]
    for copy in copies:
        copy.wait()


def gather_heads(heads):
    return pl.pallas_call(
        gather_heads_kernel,
        out_shape=jax.ShapeDtypeStruct((64, LANES), F32),
        in_specs=[pl.BlockSpec(memory_space=pltpu.VMEM)],
        out_specs=pl.BlockSpec(memory_space=pltpu.VMEM),
        scratch_shapes=[pltpu.SemaphoreType.DMA((8,)), pltpu.SemaphoreType.DMA((8,))],
        compiler_params=pltpu.CompilerParams(collective_id=0, has_side_effects=True),
        name="gather_heads",
    )(heads.reshape(8, LANES))


def lookup(table_ref, first, index):
    high = lax.shift_right_logical(index, 7) - first
    low = jnp.bitwise_and(index, 127)
    found = jnp.zeros(index.shape, F32)
    for t in range(32):
        row = jnp.broadcast_to(table_ref[pl.ds(first + t, 1), :], index.shape)
        picked = jnp.take_along_axis(row, low, axis=1, mode="promise_in_bounds")
        found = jnp.where(high == t, picked, found)
    return found


def pieces(x):
    high = x.astype(BF16).astype(F32)
    rest = x - high
    middle = rest.astype(BF16).astype(F32)
    return high, middle, rest - middle


def weirs_kernel(mask_ref, base_ref, heads_ref, coef_ref, node_ref, cell_ref, out_ref, code_ref, flux_ref):
    r = lax.axis_index("wide")
    c = lax.axis_index("narrow")
    upper = r < 8
    for j in range(2):
        col = c + 8 * j
        keep = jnp.where((mask_ref[r, col] != 0) | (r == col), 1.0, 0.0).astype(F32)
        out_ref[j] = base_ref[j] * keep
    node = node_ref[...]
    cell = cell_ref[...]
    drop = lookup(heads_ref, 0, node) - lookup(heads_ref, 32, cell)
    flux = 1.5 * coef_ref[...] * jnp.sqrt(drop * drop + 0.01)
    row = jnp.where(upper, node, cell)
    col = jnp.where(upper, cell, node)
    mine = lax.shift_right_logical(row, 9) == r
    low_row = jnp.bitwise_and(row, 511)

    target = jnp.where(upper, c + 8, c)
    slot = jnp.where(upper, 1, 0)
    hit = jnp.where(mine & (lax.shift_right_logical(col, 9) == target), 1, 0)
    code = low_row * 512 + jnp.bitwise_and(col, 511)
    steps = jnp.max(jnp.sum(hit.astype(F32), axis=0, keepdims=True)).astype(jnp.int32)
    code_ref[...] = jnp.zeros(code_ref.shape, jnp.int32)
    flux_ref[...] = jnp.zeros(flux_ref.shape, F32)
    place = lax.broadcasted_iota(jnp.int32, (ROWS, LANES), 0)

    def extract(s, left):
        first = jnp.min(jnp.where(left != 0, place, ROWS), axis=0, keepdims=True)
        now = place == first
        code_ref[pl.ds(s, 1), :] = jnp.sum(jnp.where(now, code, 0), axis=0, keepdims=True)
        flux_ref[pl.ds(s, 1), :] = jnp.sum(jnp.where(now, flux, 0.0), axis=0, keepdims=True)
        return jnp.where(now, 0, left)

    lax.fori_loop(0, steps, extract, hit)

    def scatter(b, carry):
        rows = pl.ds(pl.multiple_of(b * 8, 8), 8)
        codes = code_ref[rows]
        parts = pieces(flux_ref[rows])
        here = lax.broadcasted_iota(jnp.int32, (B, LANES), 0)
        row_of = lax.shift_right_logical(codes, 9)
        col_of = jnp.bitwise_and(codes, 511)
        right = jnp.concatenate(
            [jnp.where(here == col_of[s : s + 1], 1.0, 0.0).astype(BF16) for s in range(8)], axis=1
        )
        total = jnp.zeros((B, B), F32)
        for part in parts:
            left = jnp.concatenate(
                [jnp.where(here == row_of[s : s + 1], part[s : s + 1], 0.0).astype(BF16) for s in range(8)],
                axis=1,
            )
            total = total + dot_nt(left, right)
        out_ref[slot] = out_ref[slot] - total
        return carry

    lax.fori_loop(0, lax.div(steps + 7, 8), scatter, 0)

    @pl.when(c == lax.rem(r, 8))
    def _():
        own = jnp.where(mine, flux, 0.0)
        parts = pieces(own)
        high = lax.shift_right_logical(low_row, 7)
        low = jnp.bitwise_and(low_row, 127)
        here8 = lax.broadcasted_iota(jnp.int32, (8, LANES), 0)
        here128 = lax.broadcasted_iota(jnp.int32, (LANES, LANES), 0)
        total = jnp.zeros((24, LANES), F32)
        for g in range(ROWS // 8):
            ones = []
            lefts = []
            for s in range(8 * g, 8 * g + 8):
                ones.append(jnp.where(here128 == low[s : s + 1], 1.0, 0.0).astype(BF16))
                at = here8 == high[s : s + 1]
                lefts.append(
                    jnp.concatenate([jnp.where(at, part[s : s + 1], 0.0) for part in parts], axis=0).astype(BF16)
                )
            total = total + dot_nt(jnp.concatenate(lefts, axis=1), jnp.concatenate(ones, axis=1))
        diagonal = total[0:8] + total[8:16] + total[16:24]
        eye = here128 == lax.broadcasted_iota(jnp.int32, (LANES, LANES), 1)
        which = jnp.where(upper, 0, 1)
        for t in range(4):
            part = pl.ds(t * LANES, LANES)
            out_ref[which, part, part] = out_ref[which, part, part] + jnp.where(eye, diagonal[t : t + 1], 0.0)


def add_weirs(base, block_mask, every_head, coef, weir_node, weir_cell):
    pad = ROWS * LANES - coef.shape[0]
    coef = jnp.pad(coef, (0, pad)).reshape(ROWS, LANES)
    node = jnp.pad(weir_node, (0, pad)).reshape(ROWS, LANES)
    cell = jnp.pad(weir_cell, (0, pad), constant_values=4096).reshape(ROWS, LANES)
    vmem = pl.BlockSpec(memory_space=pltpu.VMEM)
    return pl.pallas_call(
        weirs_kernel,
        out_shape=jax.ShapeDtypeStruct((2, B, B), F32),
        in_specs=[pl.BlockSpec(memory_space=pltpu.SMEM)] + [vmem] * 5,
        out_specs=vmem,
        scratch_shapes=[pltpu.VMEM((ROWS, LANES), jnp.int32), pltpu.VMEM((ROWS, LANES), F32)],
        compiler_params=pltpu.CompilerParams(vmem_limit_bytes=VMEM_LIMIT),
        name="add_weirs",
    )(block_mask, base, every_head, coef, node, cell)


def eliminate_kernel(
    a_ref,
    out_ref,
    side,
    panel,
    direct,
    pivot,
    ph,
    pl_,
    sh,
    sl,
    xf,
    wide_send,
    wide_recv,
    pair_send,
    pair_recv,
    side_send,
    side_recv,
    direct_send,
    direct_recv,
    through_send,
    through_recv,
    last_send,
    last_recv,
):
    r = lax.axis_index("wide")
    c = lax.axis_index("narrow")
    core = lax.rem(r, 2)
    chip = lax.div(r, 2)
    y = lax.rem(chip, 4)
    x = lax.div(chip, 4)
    z = lax.rem(c, 4)
    far = lax.div(c, 4)
    up = (x * 8 + lax.rem(y + 1, 4) * 2 + core, c)
    down = (x * 8 + lax.rem(y + 3, 4) * 2 + core, c)
    across = ((1 - x) * 8 + y * 2 + core, c)
    pair = (chip * 2 + 1 - core, c)
    ahead = (r, far * 4 + lax.rem(z + 1, 4))
    behind = (r, far * 4 + lax.rem(z + 3, 4))
    over = (r, (1 - far) * 4 + z)

    barrier = pltpu.get_barrier_semaphore()
    for peer in (up, down, across, pair, ahead, behind, over):
        pl.semaphore_signal(barrier, inc=1, device_id=peer, device_id_type=MESH)
    pl.semaphore_wait(barrier, 7)

    def loop(first, last, act):
        lax.fori_loop(first, last, lambda i, carry: (act(i), carry)[1], 0)

    def pick(values, at):
        return sum(jnp.where(at == i, v, 0) for i, v in enumerate(values) if v)

    start = lambda copy: copy.start()
    sent = lambda copy: copy.wait_send()

    depth = tuple(pick(values, chip) for values in TREE_DEPTH)
    ways = tuple(tuple(pick(values, chip) == 1 for values in tree) for tree in TREE_WAYS)

    def wide_copy(j, way, target):
        rows = pl.ds(pl.multiple_of(lax.rem(j, PARTS) * CHUNK, CHUNK), CHUNK)
        chunk = panel.at[core, lax.div(j, PARTS), rows]
        return pltpu.make_async_remote_copy(
            src_ref=chunk,
            dst_ref=chunk,
            send_sem=wide_send.at[j, way],
            recv_sem=wide_recv.at[j],
            device_id=target,
            device_id_type=MESH,
        )

    def wide_each(tree, j, act):
        for way, target in enumerate((up, down, across)):

            @pl.when(ways[tree][way])
            def _():
                act(wide_copy(j, way, target))

    def wide_slot(first, end, slot, forward=False):
        for tree in range(3):
            j = 3 * (slot - SLOTS * depth[tree]) + tree

            @pl.when((j >= first) & (j < end))
            def _():
                wide_copy(j, 0, up).wait_recv()
                wide_each(tree, j, start)
                if forward:
                    last_copy(j).start()

    def wide_relay(first_block, end_block, forward=False):
        first, end = first_block * PARTS, end_block * PARTS
        loop(first // 3 - 1, (end + 2) // 3 + 4 * SLOTS, lambda slot: wide_slot(first, end, slot, forward))

    def wide_source(block, act):
        def one(j):
            for tree in range(3):

                @pl.when(lax.rem(j, 3) == tree)
                def _():
                    wide_each(tree, j, act)

        loop(block * PARTS, (block + 1) * PARTS, one)

    def pair_copy(b):
        block = panel.at[core, b]
        return pltpu.make_async_remote_copy(
            src_ref=block,
            dst_ref=block,
            send_sem=pair_send.at[b],
            recv_sem=pair_recv.at[b],
            device_id=pair,
            device_id_type=MESH,
        )

    def pair_wait(b):
        block = panel.at[1 - core, b]
        pltpu.make_async_remote_copy(
            src_ref=block,
            dst_ref=block,
            send_sem=pair_send.at[b],
            recv_sem=pair_recv.at[b],
            device_id=pair,
            device_id_type=MESH,
        ).wait_recv()

    def last_copy(j):
        rows = pl.ds(pl.multiple_of(lax.rem(j, PARTS) * CHUNK, CHUNK), CHUNK)
        chunk = panel.at[0, 3, rows]
        return pltpu.make_async_remote_copy(
            src_ref=chunk,
            dst_ref=chunk,
            send_sem=last_send.at[lax.rem(j, PARTS)],
            recv_sem=last_recv.at[lax.rem(j, PARTS)],
            device_id=pair,
            device_id_type=MESH,
        )

    def side_copy(s, j, way, target):
        chunk = side.at[s, pl.ds(pl.multiple_of(j * CHUNK, CHUNK), CHUNK)]
        return pltpu.make_async_remote_copy(
            src_ref=chunk,
            dst_ref=chunk,
            send_sem=side_send.at[s, j, way],
            recv_sem=side_recv.at[s, j],
            device_id=target,
            device_id_type=MESH,
        )

    places = tuple(far * 4 + lax.rem(z + 4 - s, 4) for s in range(2))
    side_depth = [[pick(values, place) for values in TREE_DEPTH] for place in places]
    side_ways = [
        [[pick(values, place) for values in tree] for tree in TREE_WAYS] for place in places
    ]

    def side_each(s, tree, j, act):
        for way, target in enumerate((ahead, behind, over)):

            @pl.when(side_ways[s][tree][way] == 1)
            def _():
                act(side_copy(s, j, way, target))

    def side_slot(slot):
        for s in range(2):
            for tree in range(3):
                j = 3 * (slot - 3 * s - SLOTS * side_depth[s][tree]) + tree

                @pl.when((j >= 0) & (j < PARTS))
                def _():
                    @pl.when(c != s)
                    def _():
                        side_copy(s, j, 0, ahead).wait_recv()

                    side_each(s, tree, j, start)

    SIDE_END = 6 + 4 * SLOTS

    def through_copy(b, j, way, target):
        chunk = panel.at[core, b, pl.ds(pl.multiple_of(j * CHUNK, CHUNK), CHUNK)]
        return pltpu.make_async_remote_copy(
            src_ref=chunk,
            dst_ref=chunk,
            send_sem=through_send.at[b - 2, j, way],
            recv_sem=through_recv.at[b - 2, j],
            device_id=target,
            device_id_type=MESH,
        )

    def through_each(b, s, tree, j, act):
        for way, target in enumerate((ahead, behind, over)):

            @pl.when(side_ways[s][tree][way] == 1)
            def _():
                act(through_copy(b, j, way, target))

    def through_slot(b, s, slot):
        for tree in range(3):
            j = 3 * (slot - SLOTS * side_depth[s][tree]) + tree

            @pl.when((j >= 0) & (j < PARTS))
            def _():
                @pl.when(c != s)
                def _():
                    through_copy(b, j, 0, ahead).wait_recv()

                through_each(b, s, tree, j, start)
                for kind in range(3):

                    @pl.when(lax.rem(b * PARTS + j, 3) == kind)
                    def _():
                        wide_each(kind, b * PARTS + j, start)

    THROUGH_END = (PARTS + 2) // 3 + 4 * SLOTS

    def through(b):
        loop(0, THROUGH_END, lambda slot: through_slot(b, 0, slot))

    def through_sent(b, s):
        def one(j):
            for tree in range(3):

                @pl.when(lax.rem(j, 3) == tree)
                def _():
                    through_each(b, s, tree, j, sent)

        loop(0, PARTS, one)

    def put(index, value):
        high, low = split(value)
        ph[index] = high
        pl_[index] = low

    def times(i, j):
        return product(ph[i], pl_[i], ph[j], pl_[j])

    def invert():
        here = lax.broadcasted_iota(jnp.int32, (B, B), 0) == lax.broadcasted_iota(jnp.int32, (B, B), 1)
        block = pivot[...]
        only = jnp.where(here, block, 0.0)
        one_row = 1.0 / jnp.sum(only, axis=0, keepdims=True)
        one_col = 1.0 / jnp.sum(only, axis=1, keepdims=True)
        eye = jnp.where(here, 1.0, 0.0)
        rest = eye - block * one_row
        xf[...] = one_col * (eye + rest)
        high, low = split(rest)
        sh[0, B:] = high
        sl[0, B:] = low
        high, low = split(product(sh[0, B:], sl[0, B:], sh[0, B:], sl[0, B:]))
        sh[1, B:] = high
        sl[1, B:] = low
        high, low = split(xf[...])
        sh[1, :B] = high
        sl[1, :B] = low

        def step(k):
            now = lax.rem(k, 2)
            later = 1 - now
            both = product(sh[now], sl[now], sh[now, B:], sl[now, B:])
            total = xf[...] + both[:B]
            xf[...] = total
            high, low = split(total)
            sh[later, :B] = high
            sl[later, :B] = low
            high, low = split(both[B:])
            sh[later, B:] = high
            sl[later, B:] = low

        loop(1, NS_STEPS - 1, step)
        now = (NS_STEPS - 1) % 2
        return xf[...] + product(sh[now, :B], sl[now, :B], sh[now, B:], sl[now, B:])

    def direct_copy(src, dst, at, target):
        return pltpu.make_async_remote_copy(
            src_ref=src,
            dst_ref=dst,
            send_sem=direct_send.at[at],
            recv_sem=direct_recv.at[at],
            device_id=target,
            device_id_type=MESH,
        )

    first_copy = direct_copy(a_ref.at[0], direct.at[0], 0, behind)
    second_copy = direct_copy(direct.at[1], direct.at[1], 1, behind)
    corner_copy = direct_copy(a_ref.at[0], direct.at[1], 2, pair)
    cross_copy = direct_copy(a_ref.at[0], panel.at[1, 3], 3, pair)

    @pl.when((r == 1) & (c == 1))
    def _():
        corner_copy.start()

    @pl.when((r == 0) & (c == 1))
    def _():
        cross_copy.start()
        first_copy.start()
        corner_copy.wait_recv()
        second_copy.start()

    @pl.when((r == 1) & (c == 0))
    def _():
        panel[1, 2] = a_ref[0]
        pair_copy(2).start()

    @pl.when(r < 2)
    def _():
        panel[core, 0] = a_ref[0]
        panel[core, 1] = a_ref[1]

        @pl.when(r == 0)
        def _():
            pair_copy(0).start()
            pair_copy(1).start()

        wide_source(0, start)
        wide_source(1, start)

    @pl.when((r == 0) & (c == 0))
    def _():
        pivot[...] = a_ref[0]
        first = invert()
        panel[0, 2] = first
        through(2)
        pair_copy(2).start()
        put(0, first)
        first_copy.wait_recv()
        put(1, direct[0])
        put(2, times(0, 1))
        pair_wait(2)
        put(3, panel[1, 2])
        second_copy.wait_recv()
        pivot[...] = direct[1] - times(3, 2)
        panel[0, 3] = invert()
        through(3)
        loop(0, PARTS, lambda j: last_copy(j).start())

    @pl.when((r == 0) & (c != 0))
    def _():
        through(2)
        pair_copy(2).start()
        through(3)
        loop(0, PARTS, lambda j: last_copy(j).start())

    @pl.when(r == 0)
    def _():
        put(0, panel[0, 2])
        for j in range(2):
            put(1, a_ref[j])
            out_ref[j] = times(0, 1)

    @pl.when(r == 1)
    def _():
        @pl.when(c == 1)
        def _():
            cross_copy.wait_recv()

        def both(slot):
            through_slot(2, 0, slot)
            through_slot(3, 1, slot - 1)

        loop(0, THROUGH_END + 1, both)
        put(3, panel[1, 2])

    @pl.when(r >= 2)
    def _():
        for s in range(2):

            @pl.when(c == s)
            def _():
                side[s] = a_ref[0]

        def early(slot):
            side_slot(slot)
            wide_slot(0, 2 * PARTS, slot)

        loop(0, SIDE_END, early)
        pair_copy(0).start()
        pair_copy(1).start()
        put(3, side[0])

    @pl.when((r >= 2) & (core == 0))
    def _():
        wide_relay(2, 3)
        pair_copy(2).start()
        for b in range(3):
            pair_wait(b)

    @pl.when((r >= 2) & (core == 1))
    def _():
        wide_relay(2, 4)
        pair_copy(2).start()
        pair_copy(3).start()

    @pl.when(core == 1)
    def _():
        for b in range(3):
            pair_wait(b)

    last_first = jnp.where((core == 0) & (r >= 2), 3 * PARTS, 4 * PARTS)

    def last_slot(slot):
        wide_slot(last_first, 4 * PARTS, slot, forward=True)

    def scaled_row(j):
        put(1, panel[0, j])
        put(4 + j, times(0, 1))

    def kept_row(j):
        kept = a_ref[j] - times(3, 4 + j)
        out_ref[j] = kept

        @pl.when(r == 1)
        def _():
            put(6 + j, kept)

    def first_rest(j):
        @pl.when(r >= 2)
        def _():
            if j == 0:
                put(1, panel[1, 2])
            put(6 + j, panel[1, j] - times(1, 4 + j))

    def corner_row():
        @pl.when(r >= 2)
        def _():
            @pl.when(core == 0)
            def _():
                pair_wait(3)

            put(1, panel[1, 3])
            put(2, times(0, 1))

    def column():
        @pl.when(r >= 2)
        def _():
            put(4, side[1] - times(3, 2))

    @pl.when(r >= 1)
    def _():
        put(0, panel[0, 2])
        work = [
            lambda: scaled_row(0),
            lambda: scaled_row(1),
            lambda: kept_row(0),
            lambda: kept_row(1),
            lambda: first_rest(0),
            lambda: first_rest(1),
            corner_row,
            column,
        ]
        base = 3 * PARTS // 3
        slots = list(range(base, base + 3 + 4 * SLOTS + 1))
        for k, slot in enumerate(slots):
            last_slot(slot)
            if k < len(work):
                work[k]()

        @pl.when(core == 1)
        def _():
            loop(0, PARTS, lambda j: last_copy(j).wait_recv())

        put(0, panel[0, 3])

        @pl.when(r >= 2)
        def _():
            put(0, times(4, 0))

        for j in range(2):
            scaled = times(0, 6 + j)
            live = c >= 2 if j == 0 else c >= 0

            @pl.when((r == 1) & live)
            def _():
                out_ref[j] = scaled

            @pl.when((r >= 2) & live)
            def _():
                out_ref[j] = out_ref[j] - scaled

    @pl.when(c == 0)
    def _():
        out_ref[0] = a_ref[0]

    for b in range(4):
        wide_source(b, sent)

    @pl.when(r < 2)
    def _():
        through_sent(2, 0)

    @pl.when(r == 0)
    def _():
        through_sent(3, 0)

        @pl.when(c == 1)
        def _():
            cross_copy.wait_send()
            first_copy.wait_send()
            second_copy.wait_send()

    @pl.when(r == 1)
    def _():
        through_sent(3, 1)

        @pl.when(c == 0)
        def _():
            pair_copy(2).wait_send()

        @pl.when(c == 1)
        def _():
            corner_copy.wait_send()

    @pl.when(core == 0)
    def _():
        for b in range(3):
            pair_copy(b).wait_send()
        loop(0, PARTS, lambda j: last_copy(j).wait_send())

    @pl.when(r >= 2)
    def _():
        @pl.when(core == 1)
        def _():
            for b in range(4):
                pair_copy(b).wait_send()

        for s in range(2):

            def one(j):
                for tree in range(3):

                    @pl.when(lax.rem(j, 3) == tree)
                    def _():
                        side_each(s, tree, j, sent)

            loop(0, PARTS, one)


def eliminate(blocks):
    vmem = pl.BlockSpec(memory_space=pltpu.VMEM)
    dma = pltpu.SemaphoreType.DMA
    return pl.pallas_call(
        eliminate_kernel,
        out_shape=jax.ShapeDtypeStruct((2, B, B), F32),
        in_specs=[vmem],
        out_specs=vmem,
        scratch_shapes=[
            pltpu.VMEM((2, B, B), F32),
            pltpu.VMEM((2, 4, B, B), F32),
            pltpu.VMEM((2, B, B), F32),
            pltpu.VMEM((B, B), F32),
            pltpu.VMEM((8, B, B), BF16),
            pltpu.VMEM((8, B, B), BF16),
            pltpu.VMEM((2, 2 * B, B), BF16),
            pltpu.VMEM((2, 2 * B, B), BF16),
            pltpu.VMEM((B, B), F32),
            dma((4 * PARTS, 3)),
            dma((4 * PARTS,)),
            dma((4,)),
            dma((4,)),
            dma((2, PARTS, 3)),
            dma((2, PARTS)),
            dma((4,)),
            dma((4,)),
            dma((2, PARTS, 3)),
            dma((2, PARTS)),
            dma((PARTS,)),
            dma((PARTS,)),
        ],
        compiler_params=pltpu.CompilerParams(
            collective_id=1, has_side_effects=True, vmem_limit_bytes=VMEM_LIMIT
        ),
        name="eliminate",
    )(blocks)


def per_device(base, block_mask, heads, coef, weir_node, weir_cell):
    blocks = base.reshape(2, B, B)
    every_head = gather_heads(heads)
    blocks = add_weirs(blocks, block_mask, every_head, coef, weir_node, weir_cell)
    return eliminate(blocks).reshape(base.shape)


def solution(mesh):
    placed = (P(None, "wide", None, "narrow", None, None), P(), P("narrow"), P(), P(), P())
    return jax.shard_map(
        per_device,
        mesh=mesh,
        in_specs=placed,
        out_specs=P(None, "wide", None, "narrow", None, None),
        check_vma=False,
    )
```
